32 devices in a mesh: group: 2 (over x), row: 16 (over z, y, core).
Axes of the slice: x: 2, y: 2, z: 4, core: 2. Of those that a mesh axis runs over, the one named last changes fastest.
Arguments:
- omega: bfloat16 [51200, 512], P(('group', 'row')), parts along dimension 0, may hold values from -6 to 6
- child_sketch: bfloat16 [102400, 512], P(('group', 'row')), parts along dimension 0, may hold values from -12 to 12
- child_map: int32 [102400], P(('group', 'row')), parts along dimension 0, may hold values from 0 to 25599, as said below
- skel_leaf: int32 [4096], P(('group', 'row')), parts along dimension 0, may hold values from 0 to 1599, as said below
- skel_upper: int32 [16, 128], P('group'), parts along dimension 0, may hold values from 0 to 255, as said below
Outputs:
- interp_leaf: float32 [51200, 128], P(('group', 'row')), parts along dimension 0
- interp_upper: float32 [4096, 128], P(('group', 'row')), parts along dimension 0
- nested_basis: float32 [51200, 128], P(('group', 'row')), parts along dimension 0
The draws below stay inside these ranges and needn't reach their ends.
There are 2 independent parts, one for each index of `group`. The reference program is written for one: setup_inputs(seed, part) draws one part's arguments, and reference() takes and returns one part's arrays. A program takes and returns all parts, laid end to end along the dimension named above; each array names one. Nothing has to cross between parts.
Inputs may be any that keep to these rules, and one draw needn't show every extreme that they name: `child_map`: the rows of each device fall into aligned blocks of 400 rows; all rows of one block name parent rows of a single leaf (one run of 1600 rows), and the blocks of one device name distinct leaves. `skel_leaf`: the 128 numbers of one leaf are distinct local row numbers of that leaf. `skel_upper`: each row holds 128 distinct numbers.
All inputs are finite; a program needn't handle non-finite values.
Results may differ from the reference program's by a relative error of at most 0.0003.
Values may be sent and summed in bfloat16 or wider, within the bound.
A program may use at most 128 MiB of HBM per device.

```python
import jax
import jax.numpy as jnp
from jax import lax

LINE_CELLS = 400
LINES_DEV = 4
SKETCH = 512
RANK = 128
FRONT = 25600
CHILD_ROWS = 51200
CAP = 400
N_ROW = 16


def ends_and_middle(key, count, length):
    middle = jax.random.permutation(key, count - 2)[:length - 2] + 1
    ends = jnp.array([0, count - 1], jnp.int32)
    joined = jnp.concatenate([ends, middle.astype(jnp.int32)])
    return jax.random.permutation(jax.random.fold_in(key, 5), joined)


def draw_child_map(key, part):
    key = jax.random.fold_in(key, 11)
    leaf_count = LINE_CELLS * LINES_DEV
    bin_count = N_ROW // 2

    def source(number):
        own_key = jax.random.fold_in(key, number)
        order = jax.random.permutation(own_key, N_ROW).astype(jnp.int32)
        wanted = jnp.where(number == 0, N_ROW - 1, 0)
        where_wanted = jnp.argmax(order == wanted)
        rolled = jnp.roll(order, -where_wanted)
        forced = number <= 1
        order = jnp.where(forced, rolled, order)
        targets = order[:bin_count]
        offsets = jax.random.randint(jax.random.fold_in(own_key, 7), (bin_count, CAP), 0, leaf_count)
        first_value = jnp.where(number == 0, leaf_count - 1, 0)
        first = jnp.where(forced, first_value, offsets[0, 0])
        offsets = offsets.at[0, 0].set(first)
        return (targets[:, None] * leaf_count + offsets).reshape(-1)
    return jax.vmap(source)(jnp.arange(N_ROW)).reshape(-1).astype(jnp.int32)


def draw_skel_leaf(key, part):
    key = jax.random.fold_in(key, 23)
    leaf_count = LINE_CELLS * LINES_DEV

    def leaf_draw(number):
        return ends_and_middle(jax.random.fold_in(key, number), leaf_count, RANK)
    return jax.vmap(leaf_draw)(jnp.arange(N_ROW)).reshape(-1).astype(jnp.int32)


def draw_skel_upper(key, part):
    key = jax.random.fold_in(key, 37)

    def pair_draw(number):
        return ends_and_middle(jax.random.fold_in(key, number), 2 * RANK, RANK)
    return jax.vmap(pair_draw)(jnp.arange(N_ROW // 2)).astype(jnp.int32)


def block_scale(stream_key, dims, split, least, largest):
    factor_of = 1.0
    for axis_at, shards_of in split:
        heights = jax.random.uniform(jax.random.fold_in(jax.random.fold_in(stream_key, 6), axis_at), (shards_of,), jnp.float32, least / len(split), largest / len(split))
        factor_of = factor_of * jnp.repeat(jnp.exp(heights), dims[axis_at] // shards_of).reshape((-1,) + (1,) * (len(dims) - 1 - axis_at))
    return factor_of


def noise(key, shape, scale, bound, cuts=(), dtype=jnp.bfloat16):
    level = block_scale(key, shape, cuts, -0.22, 0.18) if cuts else 1.0
    values = jax.random.normal(key, shape, jnp.float32) * scale * level
    return jnp.minimum(jnp.maximum(values, -bound), bound).astype(dtype)


def setup_inputs(seed: int = 0, part: int = 0) -> dict:
    keys = jax.random.split(jax.random.key(seed), 6)
    own_keys = jax.random.split(jax.random.fold_in(keys[5], part), 6)
    omega = noise(own_keys[0], (FRONT, SKETCH), 1.0, 6.0, ((0, 16),))
    child_sketch = noise(own_keys[1], (CHILD_ROWS, SKETCH), 2.0, 12.0, ((0, 16),))
    child_map = draw_child_map(jax.random.fold_in(jax.random.fold_in(keys[5], part), 71), part)
    skel_leaf = draw_skel_leaf(jax.random.fold_in(jax.random.fold_in(keys[5], part), 71), part)
    skel_upper = draw_skel_upper(jax.random.fold_in(jax.random.fold_in(keys[5], part), 71), part)
    return dict(omega=omega, child_sketch=child_sketch, child_map=child_map, skel_leaf=skel_leaf, skel_upper=skel_upper)


def solve_fit(sketch, chosen):
    gram_matrix = jnp.dot(chosen, chosen.T, precision=lax.Precision.HIGHEST)
    factor = jnp.linalg.cholesky(gram_matrix)
    cross_terms = jnp.dot(sketch, chosen.T, precision=lax.Precision.HIGHEST)
    return jax.scipy.linalg.cho_solve((factor, True), cross_terms.T).T

def reference(omega, child_sketch, child_map, skel_leaf, skel_upper):
    leaf_count = LINE_CELLS * LINES_DEV
    by_line = omega.astype(jnp.float32).reshape(FRONT // LINE_CELLS, LINE_CELLS, SKETCH)
    padded = jnp.pad(by_line, ((1, 1), (1, 1), (0, 0)))
    stencil_image = 6.0 * by_line - padded[2:, 1:-1] - padded[:-2, 1:-1] - padded[1:-1, 2:] - padded[1:-1, :-2]
    stencil_image = stencil_image.reshape(FRONT, SKETCH)
    sketch = stencil_image + jax.ops.segment_sum(child_sketch.astype(jnp.float32), child_map, num_segments=FRONT)
    leaf_blocks = sketch.reshape(N_ROW, leaf_count, SKETCH)
    leaf_picks = skel_leaf.reshape(N_ROW, RANK)

    def leaf_pieces(pieces):
        leaf_block, picked = pieces
        chosen = jnp.take(leaf_block, picked, axis=0)
        return (solve_fit(leaf_block, chosen), chosen)
    leaf_fit, chosen_rows = lax.map(leaf_pieces, (leaf_blocks, leaf_picks))
    paired = chosen_rows.reshape(N_ROW // 2, 2 * RANK, SKETCH)

    def upper_part(pieces):
        pair_block, picked = pieces
        return solve_fit(pair_block, jnp.take(pair_block, picked, axis=0))
    upper_fit = lax.map(upper_part, (paired, skel_upper)).reshape(N_ROW, RANK, RANK)

    def nested_part(pieces):
        return jnp.dot(pieces[0], pieces[1], precision=lax.Precision.HIGHEST)
    nested_basis = lax.map(nested_part, (leaf_fit, upper_fit))
    return (leaf_fit.reshape(FRONT, RANK), upper_fit.reshape(N_ROW * RANK, RANK), nested_basis.reshape(FRONT, RANK))
```

```python
import functools

import jax
import jax.numpy as jnp
from jax import lax
from jax.experimental import pallas as pl
from jax.experimental.pallas import tpu as pltpu
from jax.sharding import PartitionSpec as P

LINE_CELLS = 400
MESH = pl.DeviceIdType.MESH
HIGHEST = lax.Precision.HIGHEST


def exact_dot(left, right):
    return jnp.dot(left, right, precision=HIGHEST, preferred_element_type=jnp.float32)


def dot_rows(left, right):
    return lax.dot_general(
        left, right, (((1,), (1,)), ((), ())), precision=HIGHEST, preferred_element_type=jnp.float32
    )


def front_kernel(
    n, inv_ref, skel_ref, child_ref, map_ref, omega_ref, cross_ref, pair_ref,
    send_rows, got_rows, send_maps, got_maps, halo, sketch, chosen,
    row_send, row_recv, map_send, map_recv, halo_send, halo_recv, pair_send, pair_recv,
):
    me = lax.axis_index("row")
    rows = sketch.shape[0]
    columns = sketch.shape[1]
    rank = chosen.shape[1]
    tile = LINE_CELLS
    parity = me % 2
    partner = me + 1 - 2 * parity

    halo[...] = jnp.zeros_like(halo)
    barrier = pltpu.get_barrier_semaphore()

    def greet(j, carry):
        pl.semaphore_signal(barrier, inc=1, device_id={"row": (me + j) % n}, device_id_type=MESH)
        return carry

    lax.fori_loop(1, n, greet, 0)
    pl.semaphore_wait(barrier, n - 1)

    def distance(i):
        return (n // 2 + (1 - 2 * (i % 2)) * (i // 2)) % n

    def row_copy(j):
        return pltpu.make_async_remote_copy(
            send_rows.at[j], got_rows.at[j], row_send.at[j], row_recv.at[j],
            device_id={"row": (me + j) % n}, device_id_type=MESH,
        )

    def map_copy(j):
        return pltpu.make_async_remote_copy(
            send_maps.at[j], got_maps.at[j], map_send.at[j], map_recv.at[j],
            device_id={"row": (me + j) % n}, device_id_type=MESH,
        )

    def halo_copy(side):
        start = rows - LINE_CELLS if side == 0 else 0
        return pltpu.make_async_remote_copy(
            omega_ref.at[pl.ds(start, LINE_CELLS)], halo.at[side], halo_send.at[side], halo_recv.at[side],
            device_id={"row": (me + 1) % n if side == 0 else (me + n - 1) % n}, device_id_type=MESH,
        )

    def local_map(to):
        block = inv_ref[to]
        return jnp.where(block >= 0, map_ref[jnp.maximum(block, 0)] - to * rows, -1)

    def send(i, carry):
        j = distance(i)
        to = (me + j) % n
        send_maps[j] = local_map(to)
        map_copy(j).start()
        send_rows[j] = child_ref[jnp.maximum(inv_ref[to], 0)]
        row_copy(j).start()
        return carry

    @pl.when(me < n - 1)
    def _():
        halo_copy(0).start()

    @pl.when(me > 0)
    def _():
        halo_copy(1).start()

    lax.fori_loop(1, n, send, 0)

    @pl.when(me < n - 1)
    def _():
        halo_copy(0).wait_send()
        halo_copy(1).wait_recv()

    @pl.when(me > 0)
    def _():
        halo_copy(1).wait_send()
        halo_copy(0).wait_recv()

    cell = lax.broadcasted_iota(jnp.int32, (LINE_CELLS, columns), 0)
    lines = rows // LINE_CELLS
    for line in range(lines):
        here = omega_ref[line * LINE_CELLS:(line + 1) * LINE_CELLS].astype(jnp.float32)
        above = halo[0] if line == 0 else omega_ref[(line - 1) * LINE_CELLS:line * LINE_CELLS]
        below = halo[1] if line == lines - 1 else omega_ref[(line + 1) * LINE_CELLS:(line + 2) * LINE_CELLS]
        left = jnp.where(cell == 0, 0.0, pltpu.roll(here, 1, 0))
        right = jnp.where(cell == LINE_CELLS - 1, 0.0, pltpu.roll(here, LINE_CELLS - 1, 0))
        sketch[line * LINE_CELLS:(line + 1) * LINE_CELLS] = (
            6.0 * here - above.astype(jnp.float32) - below.astype(jnp.float32) - left - right
        )

    def extend_add(numbers, block):
        def step(t, carry):
            start = pl.multiple_of(t * tile, 16)
            row = lax.broadcasted_iota(jnp.int32, (tile, numbers.shape[1]), 0) + start
            hot = (row == numbers).astype(jnp.float32).astype(jnp.bfloat16)
            sketch[pl.ds(start, tile)] += jnp.dot(hot, block, preferred_element_type=jnp.float32)
            return carry

        lax.fori_loop(0, rows // tile, step, 0)

    extend_add(local_map(me), child_ref[jnp.maximum(inv_ref[me], 0)])

    def receive(i, carry):
        j = distance(i)
        map_copy(j).wait()
        row_copy(j).wait()
        extend_add(got_maps[j], got_rows[j])
        return carry

    lax.fori_loop(1, n, receive, 0)

    def choose(i, carry):
        for u in range(8):
            chosen[parity, pl.ds(i * 8 + u, 1), :] = sketch[pl.ds(skel_ref[i * 8 + u], 1), :]
        return carry

    lax.fori_loop(0, rank // 8, choose, 0)
    pair_copy = pltpu.make_async_remote_copy(
        chosen.at[parity], chosen.at[parity], pair_send, pair_recv,
        device_id={"row": partner}, device_id_type=MESH,
    )
    pair_copy.start()
    own = chosen[parity]

    def cross(t, carry):
        start = pl.multiple_of(t * tile, 16)
        cross_ref[pl.ds(start, tile)] = dot_rows(sketch[pl.ds(start, tile)], own)
        return carry

    lax.fori_loop(0, rows // tile, cross, 0)
    pair_copy.wait()
    pair_ref[...] = chosen[...]


def invert_pair(first, second):
    size = first.shape[0]
    row_id = lax.broadcasted_iota(jnp.int32, (size, size), 0)
    lane_id = lax.broadcasted_iota(jnp.int32, (size, size), 1)
    matrices = [first, second]
    for k in range(size):
        for m in range(2):
            a = matrices[m]
            scale = 1.0 / a[k:k + 1, k:k + 1]
            row = jnp.where(lane_id[:1] == k, 1.0, a[k:k + 1, :]) * scale
            column = a[:, k:k + 1]
            rest = jnp.where(lane_id == k, 0.0, a) - column * row
            matrices[m] = jnp.where(row_id == k, row, rest)
    return matrices


def solve_kernel(pick_ref, side_ref, cross_ref, pair_ref, leaf_ref, upper_ref, nested_ref, picked):
    rank = picked.shape[0]
    own = pair_ref[pl.ds(pl.multiple_of(side_ref[0] * rank, rank), rank), :]

    def pick(i, carry):
        for u in range(8):
            picked[pl.ds(i * 8 + u, 1), :] = pair_ref[pl.ds(pick_ref[i * 8 + u], 1), :]
        return carry

    lax.fori_loop(0, rank // 8, pick, 0)
    upper_rows = picked[...]
    leaf_inverse, upper_inverse = invert_pair(dot_rows(own, own), dot_rows(upper_rows, upper_rows))
    upper = exact_dot(dot_rows(own, upper_rows), upper_inverse)
    upper_ref[...] = upper
    tile = LINE_CELLS

    def finish(t, carry):
        start = pl.multiple_of(t * tile, 16)
        terms = cross_ref[pl.ds(start, tile)]
        leaf = exact_dot(terms, leaf_inverse)
        leaf_ref[pl.ds(start, tile)] = leaf
        nested_ref[pl.ds(start, tile)] = exact_dot(leaf, upper)
        return carry

    lax.fori_loop(0, cross_ref.shape[0] // tile, finish, 0)


def local(omega, child_sketch, child_map, skel_leaf, skel_upper):
    rows, columns = omega.shape
    rank = skel_leaf.shape[0]
    n = lax.axis_size("row")
    position = lax.axis_index("row")
    slot = 4 * rows // n
    blocks = child_sketch.shape[0] // slot
    padded = -(-slot // 16) * 16
    child = child_sketch.reshape(blocks, slot, columns)
    maps = child_map.reshape(blocks, 1, slot)
    targets = maps[:, 0, 0] // rows
    if padded != slot:
        child = jnp.pad(child, ((0, 0), (0, padded - slot), (0, 0)))
        maps = jnp.pad(maps, ((0, 0), (0, 0), (0, padded - slot)), constant_values=-1)
    numbers = jnp.arange(blocks, dtype=jnp.int32)
    places = jnp.arange(n, dtype=jnp.int32)
    inv = jnp.max(jnp.where(targets[None, :] == places[:, None], numbers[None, :], -1), axis=1)
    vmem = pl.BlockSpec(memory_space=pltpu.VMEM)
    smem = pl.BlockSpec(memory_space=pltpu.SMEM)
    dma = pltpu.SemaphoreType.DMA
    cross, pair = pl.pallas_call(
        functools.partial(front_kernel, n),
        out_shape=(
            jax.ShapeDtypeStruct((rows, rank), jnp.float32),
            jax.ShapeDtypeStruct((2, rank, columns), jnp.float32),
        ),
        in_specs=[smem, smem, vmem, vmem, vmem],
        out_specs=(vmem, vmem),
        scratch_shapes=[
            pltpu.VMEM((n, padded, columns), jnp.bfloat16),
            pltpu.VMEM((n, padded, columns), jnp.bfloat16),
            pltpu.VMEM((n, 1, padded), jnp.int32),
            pltpu.VMEM((n, 1, padded), jnp.int32),
            pltpu.VMEM((2, LINE_CELLS, columns), jnp.bfloat16),
            pltpu.VMEM((rows, columns), jnp.float32),
            pltpu.VMEM((2, rank, columns), jnp.float32),
            dma((n,)), dma((n,)), dma((n,)), dma((n,)), dma((2,)), dma((2,)), dma, dma,
        ],
        compiler_params=pltpu.CompilerParams(
            collective_id=0, has_side_effects=True, vmem_limit_bytes=48 * 1024 * 1024
        ),
    )(inv, skel_leaf, child, maps, omega)
    picks = lax.dynamic_slice_in_dim(skel_upper, position // 2, 1, 0)[0]
    return pl.pallas_call(
        solve_kernel,
        out_shape=(
            jax.ShapeDtypeStruct((rows, rank), jnp.float32),
            jax.ShapeDtypeStruct((rank, rank), jnp.float32),
            jax.ShapeDtypeStruct((rows, rank), jnp.float32),
        ),
        in_specs=[smem, smem, vmem, vmem],
        out_specs=(vmem, vmem, vmem),
        scratch_shapes=[pltpu.VMEM((rank, columns), jnp.float32)],
        compiler_params=pltpu.CompilerParams(vmem_limit_bytes=32 * 1024 * 1024),
    )(picks, (position % 2).reshape(1), cross, pair.reshape(2 * rank, columns))


def solution(mesh):
    in_specs = (
        P(("group", "row"), None),
        P(("group", "row"), None),
        P(("group", "row")),
        P(("group", "row")),
        P("group", None),
    )
    out_specs = (P(("group", "row"), None), P(("group", "row"), None), P(("group", "row"), None))
    return jax.shard_map(local, mesh=mesh, in_specs=in_specs, out_specs=out_specs, check_vma=False)
```

```python
import functools

import jax
import jax.numpy as jnp
from jax import lax
from jax.experimental import pallas as pl
from jax.experimental.pallas import tpu as pltpu
from jax.sharding import PartitionSpec as P

LINE_CELLS = 400
LANES = 128
TILE = 320
GROUP = 64
MESH = pl.DeviceIdType.MESH
HIGHEST = lax.Precision.HIGHEST


def exact_dot(left, right):
    return jnp.dot(left, right, precision=HIGHEST, preferred_element_type=jnp.float32)


def dot_rows(left, right):
    return lax.dot_general(
        left, right, (((1,), (1,)), ((), ())), precision=HIGHEST, preferred_element_type=jnp.float32
    )


def front_kernel(
    n, inv_ref, skel_ref, child_ref, map_ref, omega_ref, cross_ref, pair_ref,
    own_rows, got_own, far_rows, got_far, send_maps, got_maps, hot, coded, got_coded, scales, got_scales,
    halo, sketch, chosen,
    own_send, own_recv, far_send, far_recv, map_send, map_recv,
    code_send, code_recv, scale_send, scale_recv, halo_send, halo_recv, pair_send, pair_recv,
):
    me = lax.axis_index("row")
    rows = sketch.shape[0]
    columns = sketch.shape[1]
    rank = chosen.shape[1]
    padded = child_ref.shape[1]
    half = n // 2
    base = me // half * half
    place = me % half
    mirror = (me + half) % n
    other = mirror // half * half
    parity = me % 2
    partner = me + 1 - 2 * parity
    chunks = columns // LANES

    halo[...] = jnp.zeros_like(halo)
    scales[...] = jnp.zeros_like(scales)
    barrier = pltpu.get_barrier_semaphore()

    def greet(j, carry):
        pl.semaphore_signal(barrier, inc=1, device_id={"row": (me + j) % n}, device_id_type=MESH)
        return carry

    lax.fori_loop(1, n, greet, 0)
    pl.semaphore_wait(barrier, n - 1)

    def peer_copy(source, target, send, recv, j):
        return pltpu.make_async_remote_copy(
            source, target, send, recv,
            device_id={"row": base + (place + j) % half}, device_id_type=MESH,
        )

    def own_copy(j):
        return peer_copy(own_rows.at[j], got_own.at[j], own_send.at[j], own_recv.at[j], j)

    def far_copy(q, j):
        return peer_copy(far_rows.at[q, j], got_far.at[q, j], far_send.at[q, j], far_recv.at[q, j], j)

    def map_copy(j):
        return peer_copy(send_maps.at[j], got_maps.at[j], map_send.at[j], map_recv.at[j], j)

    def code_copy(q):
        return pltpu.make_async_remote_copy(
            coded.at[q], got_coded.at[q], code_send.at[q], code_recv.at[q],
            device_id={"row": mirror}, device_id_type=MESH,
        )

    def scale_copy(q):
        return pltpu.make_async_remote_copy(
            scales.at[q], got_scales.at[q], scale_send.at[q], scale_recv.at[q],
            device_id={"row": mirror}, device_id_type=MESH,
        )

    def halo_copy(side):
        start = rows - LINE_CELLS if side == 0 else 0
        return pltpu.make_async_remote_copy(
            omega_ref.at[pl.ds(start, LINE_CELLS)], halo.at[side], halo_send.at[side], halo_recv.at[side],
            device_id={"row": (me + 1) % n if side == 0 else (me + n - 1) % n}, device_id_type=MESH,
        )

    def local_map(to):
        block = inv_ref[to]
        return jnp.where(block >= 0, map_ref[jnp.maximum(block, 0)] - to * rows, -1)

    def block_of(to):
        return jnp.maximum(inv_ref[to], 0)

    def send_map(j, carry):
        at = (place + j) % half
        send_maps[j, 0] = local_map(base + at)
        send_maps[j, 1] = local_map(other + at)
        map_copy(j).start()
        return carry

    def send_far(q):
        def step(j, carry):
            far_rows[q, j] = child_ref[block_of(other + (place + j) % half), :, q * LANES:(q + 1) * LANES]
            far_copy(q, j).start()
            return carry

        lax.fori_loop(1, half, step, 0)

    def send_own(j, carry):
        own_rows[j] = child_ref[block_of(base + (place + j) % half)]
        own_copy(j).start()
        return carry

    def send_group(g):
        low, high = 1 + (half - 1) * g // chunks, 1 + (half - 1) * (g + 1) // chunks
        lax.fori_loop(low, high, send_own, 0)

    lax.fori_loop(1, half, send_map, 0)
    send_far(0)

    @pl.when(me < n - 1)
    def _():
        halo_copy(0).start()

    @pl.when(me > 0)
    def _():
        halo_copy(1).start()

    for q in range(1, chunks):
        send_far(q)
    send_group(0)

    def mark(j, numbers):
        def step(t, carry):
            start = pl.multiple_of(t * TILE, 16)
            row = lax.broadcasted_iota(jnp.int32, (TILE, padded), 0) + start
            hot[j, pl.ds(start, TILE)] = (row == numbers).astype(jnp.float32).astype(jnp.bfloat16)
            return carry

        lax.fori_loop(0, rows // TILE, step, 0)

    mark(0, local_map(mirror))
    far_block = block_of(mirror)
    for q in range(chunks):
        got_far[q, 0] = child_ref[far_block, :, q * LANES:(q + 1) * LANES]

    def mark_peer(j, carry):
        map_copy(j).wait()
        mark(j, got_maps[j, 1])
        return carry

    lax.fori_loop(1, half, mark_peer, 0)

    eye = (
        lax.broadcasted_iota(jnp.int32, (GROUP, LANES), 0) == lax.broadcasted_iota(jnp.int32, (GROUP, LANES), 1)
    ).astype(jnp.float32)
    groups = TILE // GROUP

    for q in range(chunks):
        def arrived(j, carry):
            far_copy(q, j).wait()
            return carry

        lax.fori_loop(1, half, arrived, 0)

        def code(t, carry):
            start = pl.multiple_of(t * TILE, 16)

            def add(j, total):
                return total + jnp.dot(
                    hot[j, pl.ds(start, TILE)], got_far[q, j], preferred_element_type=jnp.float32
                )

            total = lax.fori_loop(0, half, add, jnp.zeros((TILE, LANES), jnp.float32))
            largest = jnp.max(jnp.abs(total), axis=1, keepdims=True)
            scale = largest * (1.0 / 32767.0)
            factor = jnp.where(largest > 0.0, 32767.0 / jnp.where(largest > 0.0, largest, 1.0), 0.0)
            whole = jnp.clip(jnp.floor(total * factor + 0.5), -32767.0, 32767.0)
            coded[q, pl.ds(start, TILE)] = whole.astype(jnp.int32).astype(jnp.int16)
            for u in range(groups):
                flat = jnp.sum(scale[u * GROUP:(u + 1) * GROUP] * eye, axis=0, keepdims=True)
                scales[q, pl.ds(t * groups + u, 1), :] = flat
            return carry

        lax.fori_loop(0, rows // TILE, code, 0)
        scale_copy(q).start()
        code_copy(q).start()
        if q + 1 < chunks:
            send_group(q + 1)

    @pl.when(me < n - 1)
    def _():
        halo_copy(0).wait_send()
        halo_copy(1).wait_recv()

    @pl.when(me > 0)
    def _():
        halo_copy(1).wait_send()
        halo_copy(0).wait_recv()

    cell = lax.broadcasted_iota(jnp.int32, (LINE_CELLS, columns), 0)
    lines = rows // LINE_CELLS
    for line in range(lines):
        here = omega_ref[line * LINE_CELLS:(line + 1) * LINE_CELLS].astype(jnp.float32)
        above = halo[0] if line == 0 else omega_ref[(line - 1) * LINE_CELLS:line * LINE_CELLS]
        below = halo[1] if line == lines - 1 else omega_ref[(line + 1) * LINE_CELLS:(line + 2) * LINE_CELLS]
        left = jnp.where(cell == 0, 0.0, pltpu.roll(here, 1, 0))
        right = jnp.where(cell == LINE_CELLS - 1, 0.0, pltpu.roll(here, LINE_CELLS - 1, 0))
        sketch[line * LINE_CELLS:(line + 1) * LINE_CELLS] = (
            6.0 * here - above.astype(jnp.float32) - below.astype(jnp.float32) - left - right
        )

    def extend_add(numbers, block):
        def step(t, carry):
            start = pl.multiple_of(t * TILE, 16)
            row = lax.broadcasted_iota(jnp.int32, (TILE, padded), 0) + start
            marks = (row == numbers).astype(jnp.float32).astype(jnp.bfloat16)
            sketch[pl.ds(start, TILE)] += jnp.dot(marks, block, preferred_element_type=jnp.float32)
            return carry

        lax.fori_loop(0, rows // TILE, step, 0)

    extend_add(local_map(me), child_ref[block_of(me)])

    def receive(j, carry):
        own_copy(j).wait()
        extend_add(got_maps[j, 0], got_own[j])
        return carry

    lax.fori_loop(1, half, receive, 0)

    for q in range(chunks):
        scale_copy(q).wait()
        code_copy(q).wait()

        def decode(t, carry):
            for u in range(groups):
                start = pl.multiple_of(t * TILE + u * GROUP, 16)
                flat = got_scales[q, pl.ds(t * groups + u, 1), :]
                scale = jnp.sum(flat * eye, axis=1, keepdims=True)
                part = got_coded[q, pl.ds(start, GROUP)].astype(jnp.int32).astype(jnp.float32) * scale
                sketch[pl.ds(start, GROUP), q * LANES:(q + 1) * LANES] += part
            return carry

        lax.fori_loop(0, rows // TILE, decode, 0)

    def choose(i, carry):
        for u in range(8):
            chosen[parity, pl.ds(i * 8 + u, 1), :] = sketch[pl.ds(skel_ref[i * 8 + u], 1), :]
        return carry

    lax.fori_loop(0, rank // 8, choose, 0)
    pair_copy = pltpu.make_async_remote_copy(
        chosen.at[parity], chosen.at[parity], pair_send, pair_recv,
        device_id={"row": partner}, device_id_type=MESH,
    )
    pair_copy.start()
    own = chosen[parity]

    def cross(t, carry):
        start = pl.multiple_of(t * TILE, 16)
        cross_ref[pl.ds(start, TILE)] = dot_rows(sketch[pl.ds(start, TILE)], own)
        return carry

    lax.fori_loop(0, rows // TILE, cross, 0)
    pair_copy.wait()
    pair_ref[...] = chosen[...]


def invert_pair(first, second):
    size = first.shape[0]
    row_id = lax.broadcasted_iota(jnp.int32, (size, size), 0)
    lane_id = lax.broadcasted_iota(jnp.int32, (size, size), 1)
    matrices = [first, second]
    for k in range(size):
        for m in range(2):
            a = matrices[m]
            scale = 1.0 / a[k:k + 1, k:k + 1]
            row = jnp.where(lane_id[:1] == k, 1.0, a[k:k + 1, :]) * scale
            column = a[:, k:k + 1]
            rest = jnp.where(lane_id == k, 0.0, a) - column * row
            matrices[m] = jnp.where(row_id == k, row, rest)
    return matrices


def solve_kernel(pick_ref, side_ref, cross_ref, pair_ref, leaf_ref, upper_ref, nested_ref, picked):
    rank = picked.shape[0]
    own = pair_ref[pl.ds(pl.multiple_of(side_ref[0] * rank, rank), rank), :]

    def pick(i, carry):
        for u in range(8):
            picked[pl.ds(i * 8 + u, 1), :] = pair_ref[pl.ds(pick_ref[i * 8 + u], 1), :]
        return carry

    lax.fori_loop(0, rank // 8, pick, 0)
    upper_rows = picked[...]
    leaf_inverse, upper_inverse = invert_pair(dot_rows(own, own), dot_rows(upper_rows, upper_rows))
    upper = exact_dot(dot_rows(own, upper_rows), upper_inverse)
    upper_ref[...] = upper
    tile = LINE_CELLS

    def finish(t, carry):
        start = pl.multiple_of(t * tile, 16)
        terms = cross_ref[pl.ds(start, tile)]
        leaf = exact_dot(terms, leaf_inverse)
        leaf_ref[pl.ds(start, tile)] = leaf
        nested_ref[pl.ds(start, tile)] = exact_dot(leaf, upper)
        return carry

    lax.fori_loop(0, cross_ref.shape[0] // tile, finish, 0)


def local(omega, child_sketch, child_map, skel_leaf, skel_upper):
    rows, columns = omega.shape
    rank = skel_leaf.shape[0]
    n = lax.axis_size("row")
    position = lax.axis_index("row")
    slot = 4 * rows // n
    blocks = child_sketch.shape[0] // slot
    padded = -(-slot // 16) * 16
    child = child_sketch.reshape(blocks, slot, columns)
    maps = child_map.reshape(blocks, 1, slot)
    targets = maps[:, 0, 0] // rows
    if padded != slot:
        child = jnp.pad(child, ((0, 0), (0, padded - slot), (0, 0)))
        maps = jnp.pad(maps, ((0, 0), (0, 0), (0, padded - slot)), constant_values=-1)
    numbers = jnp.arange(blocks, dtype=jnp.int32)
    places = jnp.arange(n, dtype=jnp.int32)
    inv = jnp.max(jnp.where(targets[None, :] == places[:, None], numbers[None, :], -1), axis=1)
    vmem = pl.BlockSpec(memory_space=pltpu.VMEM)
    smem = pl.BlockSpec(memory_space=pltpu.SMEM)
    dma = pltpu.SemaphoreType.DMA
    half, chunks = n // 2, columns // LANES
    scale_rows = -(-rows // (GROUP * 8)) * 8
    cross, pair = pl.pallas_call(
        functools.partial(front_kernel, n),
        out_shape=(
            jax.ShapeDtypeStruct((rows, rank), jnp.float32),
            jax.ShapeDtypeStruct((2, rank, columns), jnp.float32),
        ),
        in_specs=[smem, smem, vmem, vmem, vmem],
        out_specs=(vmem, vmem),
        scratch_shapes=[
            pltpu.VMEM((half, padded, columns), jnp.bfloat16),
            pltpu.VMEM((half, padded, columns), jnp.bfloat16),
            pltpu.VMEM((chunks, half, padded, LANES), jnp.bfloat16),
            pltpu.VMEM((chunks, half, padded, LANES), jnp.bfloat16),
            pltpu.VMEM((half, 2, 1, padded), jnp.int32),
            pltpu.VMEM((half, 2, 1, padded), jnp.int32),
            pltpu.VMEM((half, rows, padded), jnp.bfloat16),
            pltpu.VMEM((chunks, rows, LANES), jnp.int16),
            pltpu.VMEM((chunks, rows, LANES), jnp.int16),
            pltpu.VMEM((chunks, scale_rows, LANES), jnp.float32),
            pltpu.VMEM((chunks, scale_rows, LANES), jnp.float32),
            pltpu.VMEM((2, LINE_CELLS, columns), jnp.bfloat16),
            pltpu.VMEM((rows, columns), jnp.float32),
            pltpu.VMEM((2, rank, columns), jnp.float32),
            dma((half,)), dma((half,)), dma((chunks, half)), dma((chunks, half)), dma((half,)), dma((half,)),
            dma((chunks,)), dma((chunks,)), dma((chunks,)), dma((chunks,)), dma((2,)), dma((2,)), dma, dma,
        ],
        compiler_params=pltpu.CompilerParams(
            collective_id=0, has_side_effects=True, vmem_limit_bytes=56 * 1024 * 1024
        ),
    )(inv, skel_leaf, child, maps, omega)
    picks = lax.dynamic_slice_in_dim(skel_upper, position // 2, 1, 0)[0]
    return pl.pallas_call(
        solve_kernel,
        out_shape=(
            jax.ShapeDtypeStruct((rows, rank), jnp.float32),
            jax.ShapeDtypeStruct((rank, rank), jnp.float32),
            jax.ShapeDtypeStruct((rows, rank), jnp.float32),
        ),
        in_specs=[smem, smem, vmem, vmem],
        out_specs=(vmem, vmem, vmem),
        scratch_shapes=[pltpu.VMEM((rank, columns), jnp.float32)],
        compiler_params=pltpu.CompilerParams(vmem_limit_bytes=32 * 1024 * 1024),
    )(picks, (position % 2).reshape(1), cross, pair.reshape(2 * rank, columns))


def solution(mesh):
    in_specs = (
        P(("group", "row"), None),
        P(("group", "row"), None),
        P(("group", "row")),
        P(("group", "row")),
        P("group", None),
    )
    out_specs = (P(("group", "row"), None), P(("group", "row"), None), P(("group", "row"), None))
    return jax.shard_map(local, mesh=mesh, in_specs=in_specs, out_specs=out_specs, check_vma=False)
```

```python
import functools

import jax
import jax.numpy as jnp
from jax import lax
from jax.experimental import pallas as pl
from jax.experimental.pallas import tpu as pltpu
from jax.sharding import PartitionSpec as P

LINE_CELLS = 400
LANES = 128
TILE = 320
GROUP = 64
MESH = pl.DeviceIdType.MESH
HIGHEST = lax.Precision.HIGHEST


def exact_dot(left, right):
    return jnp.dot(left, right, precision=HIGHEST, preferred_element_type=jnp.float32)


def dot_rows(left, right):
    return lax.dot_general(
        left, right, (((1,), (1,)), ((), ())), precision=HIGHEST, preferred_element_type=jnp.float32
    )


def front_kernel(
    n, inv_ref, skel_ref, child_ref, map_ref, omega_ref, cross_ref, pair_ref,
    own_rows, got_own, far_rows, got_far, send_maps, got_maps, hot, coded, got_coded, scales, got_scales,
    halo, sketch, chosen,
    own_send, own_recv, far_send, far_recv, map_send, map_recv,
    code_send, code_recv, scale_send, scale_recv, halo_send, halo_recv, pair_send, pair_recv,
):
    me = lax.axis_index("row")
    rows = sketch.shape[0]
    columns = sketch.shape[1]
    rank = chosen.shape[1]
    padded = child_ref.shape[1]
    half = n // 2
    base = me // half * half
    place = me % half
    mirror = (me + half) % n
    other = mirror // half * half
    parity = me % 2
    partner = me + 1 - 2 * parity
    chunks = columns // LANES

    halo[...] = jnp.zeros_like(halo)
    scales[...] = jnp.zeros_like(scales)
    barrier = pltpu.get_barrier_semaphore()

    def greet(j, carry):
        pl.semaphore_signal(barrier, inc=1, device_id={"row": (me + j) % n}, device_id_type=MESH)
        return carry

    lax.fori_loop(1, n, greet, 0)
    pl.semaphore_wait(barrier, n - 1)

    def peer_copy(source, target, send, recv, j):
        return pltpu.make_async_remote_copy(
            source, target, send, recv,
            device_id={"row": base + (place + j) % half}, device_id_type=MESH,
        )

    def own_copy(j):
        return peer_copy(own_rows.at[j], got_own.at[j], own_send.at[j], own_recv.at[j], j)

    def far_copy(q, j):
        return peer_copy(far_rows.at[q, j], got_far.at[q, j], far_send.at[q, j], far_recv.at[q, j], j)

    def map_copy(j):
        return peer_copy(send_maps.at[j], got_maps.at[j], map_send.at[j], map_recv.at[j], j)

    def code_copy(q):
        return pltpu.make_async_remote_copy(
            coded.at[q], got_coded.at[q], code_send.at[q], code_recv.at[q],
            device_id={"row": mirror}, device_id_type=MESH,
        )

    def scale_copy(q):
        return pltpu.make_async_remote_copy(
            scales.at[q], got_scales.at[q], scale_send.at[q], scale_recv.at[q],
            device_id={"row": mirror}, device_id_type=MESH,
        )

    def halo_copy(side):
        start = rows - LINE_CELLS if side == 0 else 0
        return pltpu.make_async_remote_copy(
            omega_ref.at[pl.ds(start, LINE_CELLS)], halo.at[side], halo_send.at[side], halo_recv.at[side],
            device_id={"row": (me + 1) % n if side == 0 else (me + n - 1) % n}, device_id_type=MESH,
        )

    def local_map(to):
        block = inv_ref[to]
        return jnp.where(block >= 0, map_ref[jnp.maximum(block, 0)] - to * rows, -1)

    def block_of(to):
        return jnp.maximum(inv_ref[to], 0)

    def send_map(j, carry):
        at = (place + j) % half
        send_maps[j, 0] = local_map(base + at)
        send_maps[j, 1] = local_map(other + at)
        map_copy(j).start()
        return carry

    def send_far(q):
        def step(j, carry):
            far_rows[q, j] = child_ref[block_of(other + (place + j) % half), :, q * LANES:(q + 1) * LANES]
            far_copy(q, j).start()
            return carry

        lax.fori_loop(1, half, step, 0)

    def send_own(j, carry):
        own_rows[j] = child_ref[block_of(base + (place + j) % half)]
        own_copy(j).start()
        return carry

    def send_group(g):
        low, high = 1 + (half - 1) * g // chunks, 1 + (half - 1) * (g + 1) // chunks
        lax.fori_loop(low, high, send_own, 0)

    lax.fori_loop(1, half, send_map, 0)
    send_far(0)

    @pl.when(me < n - 1)
    def _():
        halo_copy(0).start()

    @pl.when(me > 0)
    def _():
        halo_copy(1).start()

    for q in range(1, chunks):
        send_far(q)
    send_group(0)

    def mark(j, numbers):
        def step(t, carry):
            start = pl.multiple_of(t * TILE, 16)
            row = lax.broadcasted_iota(jnp.int32, (TILE, padded), 0) + start
            hot[j, pl.ds(start, TILE)] = (row == numbers).astype(jnp.float32).astype(jnp.bfloat16)
            return carry

        lax.fori_loop(0, rows // TILE, step, 0)

    mark(0, local_map(mirror))
    far_block = block_of(mirror)
    for q in range(chunks):
        got_far[q, 0] = child_ref[far_block, :, q * LANES:(q + 1) * LANES]

    def mark_peer(j, carry):
        map_copy(j).wait()
        mark(j, got_maps[j, 1])
        return carry

    lax.fori_loop(1, half, mark_peer, 0)

    eye = (
        lax.broadcasted_iota(jnp.int32, (GROUP, LANES), 0) == lax.broadcasted_iota(jnp.int32, (GROUP, LANES), 1)
    ).astype(jnp.float32)
    groups = TILE // GROUP

    for q in range(chunks):
        def arrived(j, carry):
            far_copy(q, j).wait()
            return carry

        lax.fori_loop(1, half, arrived, 0)

        def code(t, carry):
            start = pl.multiple_of(t * TILE, 16)

            def add(j, total):
                return total + jnp.dot(
                    hot[j, pl.ds(start, TILE)], got_far[q, j], preferred_element_type=jnp.float32
                )

            total = lax.fori_loop(0, half, add, jnp.zeros((TILE, LANES), jnp.float32))
            largest = jnp.max(jnp.abs(total), axis=1, keepdims=True)
            scale = largest * (1.0 / 32767.0)
            factor = jnp.where(largest > 0.0, 32767.0 / jnp.where(largest > 0.0, largest, 1.0), 0.0)
            whole = jnp.clip(jnp.floor(total * factor + 0.5), -32767.0, 32767.0)
            coded[q, pl.ds(start, TILE)] = whole.astype(jnp.int32).astype(jnp.int16)
            for u in range(groups):
                flat = jnp.sum(scale[u * GROUP:(u + 1) * GROUP] * eye, axis=0, keepdims=True)
                scales[q, pl.ds(t * groups + u, 1), :] = flat
            return carry

        lax.fori_loop(0, rows // TILE, code, 0)
        scale_copy(q).start()
        code_copy(q).start()
        if q + 1 < chunks:
            send_group(q + 1)

    @pl.when(me < n - 1)
    def _():
        halo_copy(0).wait_send()
        halo_copy(1).wait_recv()

    @pl.when(me > 0)
    def _():
        halo_copy(1).wait_send()
        halo_copy(0).wait_recv()

    cell = lax.broadcasted_iota(jnp.int32, (LINE_CELLS, columns), 0)
    lines = rows // LINE_CELLS
    for line in range(lines):
        here = omega_ref[line * LINE_CELLS:(line + 1) * LINE_CELLS].astype(jnp.float32)
        above = halo[0] if line == 0 else omega_ref[(line - 1) * LINE_CELLS:line * LINE_CELLS]
        below = halo[1] if line == lines - 1 else omega_ref[(line + 1) * LINE_CELLS:(line + 2) * LINE_CELLS]
        left = jnp.where(cell == 0, 0.0, pltpu.roll(here, 1, 0))
        right = jnp.where(cell == LINE_CELLS - 1, 0.0, pltpu.roll(here, LINE_CELLS - 1, 0))
        sketch[line * LINE_CELLS:(line + 1) * LINE_CELLS] = (
            6.0 * here - above.astype(jnp.float32) - below.astype(jnp.float32) - left - right
        )

    mark(0, local_map(me))

    def mark_own(j, carry):
        mark(j, got_maps[j, 0])
        return carry

    lax.fori_loop(1, half, mark_own, 0)

    def extend_add(j, block):
        def step(t, carry):
            start = pl.multiple_of(t * TILE, 16)
            sketch[pl.ds(start, TILE)] += jnp.dot(
                hot[j, pl.ds(start, TILE)], block, preferred_element_type=jnp.float32
            )
            return carry

        lax.fori_loop(0, rows // TILE, step, 0)

    extend_add(0, child_ref[block_of(me)])

    def receive(j, carry):
        own_copy(j).wait()
        extend_add(j, got_own[j])
        return carry

    lax.fori_loop(1, half - half // 4, receive, 0)

    for q in range(chunks):
        if q == chunks // 2:
            lax.fori_loop(half - half // 4, half, receive, 0)
        scale_copy(q).wait()
        code_copy(q).wait()

        def decode(t, carry):
            for u in range(groups):
                start = pl.multiple_of(t * TILE + u * GROUP, 16)
                flat = got_scales[q, pl.ds(t * groups + u, 1), :]
                scale = jnp.sum(flat * eye, axis=1, keepdims=True)
                part = got_coded[q, pl.ds(start, GROUP)].astype(jnp.int32).astype(jnp.float32) * scale
                sketch[pl.ds(start, GROUP), q * LANES:(q + 1) * LANES] += part
            return carry

        lax.fori_loop(0, rows // TILE, decode, 0)

    def choose(i, carry):
        for u in range(8):
            chosen[parity, pl.ds(i * 8 + u, 1), :] = sketch[pl.ds(skel_ref[i * 8 + u], 1), :]
        return carry

    lax.fori_loop(0, rank // 8, choose, 0)
    pair_copy = pltpu.make_async_remote_copy(
        chosen.at[parity], chosen.at[parity], pair_send, pair_recv,
        device_id={"row": partner}, device_id_type=MESH,
    )
    pair_copy.start()
    own = chosen[parity]

    def cross(t, carry):
        start = pl.multiple_of(t * TILE, 16)
        cross_ref[pl.ds(start, TILE)] = dot_rows(sketch[pl.ds(start, TILE)], own)
        return carry

    lax.fori_loop(0, rows // TILE, cross, 0)
    pair_copy.wait()
    pair_ref[...] = chosen[...]


def invert_pair(first, second):
    size = first.shape[0]
    row_id = lax.broadcasted_iota(jnp.int32, (size, size), 0)
    lane_id = lax.broadcasted_iota(jnp.int32, (size, size), 1)
    matrices = [first, second]
    for k in range(size):
        for m in range(2):
            a = matrices[m]
            scale = 1.0 / a[k:k + 1, k:k + 1]
            row = jnp.where(lane_id[:1] == k, 1.0, a[k:k + 1, :]) * scale
            column = a[:, k:k + 1]
            rest = jnp.where(lane_id == k, 0.0, a) - column * row
            matrices[m] = jnp.where(row_id == k, row, rest)
    return matrices


def gram_blocks(rows):
    half = rows.shape[0] // 2
    top, low = rows[:half], rows[half:]
    return dot_rows(top, top), dot_rows(top, low), dot_rows(low, top), dot_rows(low, low)


def invert_grams(first, second):
    blocks = [gram_blocks(first), gram_blocks(second)]
    tops = invert_pair(blocks[0][0], blocks[1][0])
    left = [exact_dot(b[2], p) for b, p in zip(blocks, tops)]
    right = [exact_dot(p, b[1]) for b, p in zip(blocks, tops)]
    lows = invert_pair(*[b[3] - exact_dot(v, b[1]) for b, v in zip(blocks, left)])
    inverses = []
    for p, q, v, w in zip(tops, lows, left, right):
        low_left = -exact_dot(q, v)
        top = jnp.concatenate([p - exact_dot(w, low_left), -exact_dot(w, q)], axis=1)
        inverses.append(jnp.concatenate([top, jnp.concatenate([low_left, q], axis=1)], axis=0))
    return inverses


def solve_kernel(pick_ref, side_ref, cross_ref, pair_ref, leaf_ref, upper_ref, nested_ref, picked):
    rank = picked.shape[0]
    own = pair_ref[pl.ds(pl.multiple_of(side_ref[0] * rank, rank), rank), :]

    def pick(i, carry):
        for u in range(8):
            picked[pl.ds(i * 8 + u, 1), :] = pair_ref[pl.ds(pick_ref[i * 8 + u], 1), :]
        return carry

    lax.fori_loop(0, rank // 8, pick, 0)
    upper_rows = picked[...]
    leaf_inverse, upper_inverse = invert_grams(own, upper_rows)
    upper = exact_dot(dot_rows(own, upper_rows), upper_inverse)
    upper_ref[...] = upper
    tile = LINE_CELLS

    def finish(t, carry):
        start = pl.multiple_of(t * tile, 16)
        terms = cross_ref[pl.ds(start, tile)]
        leaf = exact_dot(terms, leaf_inverse)
        leaf_ref[pl.ds(start, tile)] = leaf
        nested_ref[pl.ds(start, tile)] = exact_dot(leaf, upper)
        return carry

    lax.fori_loop(0, cross_ref.shape[0] // tile, finish, 0)


def local(omega, child_sketch, child_map, skel_leaf, skel_upper):
    rows, columns = omega.shape
    rank = skel_leaf.shape[0]
    n = lax.axis_size("row")
    position = lax.axis_index("row")
    slot = 4 * rows // n
    blocks = child_sketch.shape[0] // slot
    padded = -(-slot // 16) * 16
    child = child_sketch.reshape(blocks, slot, columns)
    maps = child_map.reshape(blocks, 1, slot)
    targets = maps[:, 0, 0] // rows
    if padded != slot:
        child = jnp.pad(child, ((0, 0), (0, padded - slot), (0, 0)))
        maps = jnp.pad(maps, ((0, 0), (0, 0), (0, padded - slot)), constant_values=-1)
    numbers = jnp.arange(blocks, dtype=jnp.int32)
    places = jnp.arange(n, dtype=jnp.int32)
    inv = jnp.max(jnp.where(targets[None, :] == places[:, None], numbers[None, :], -1), axis=1)
    vmem = pl.BlockSpec(memory_space=pltpu.VMEM)
    smem = pl.BlockSpec(memory_space=pltpu.SMEM)
    dma = pltpu.SemaphoreType.DMA
    half, chunks = n // 2, columns // LANES
    scale_rows = -(-rows // (GROUP * 8)) * 8
    cross, pair = pl.pallas_call(
        functools.partial(front_kernel, n),
        out_shape=(
            jax.ShapeDtypeStruct((rows, rank), jnp.float32),
            jax.ShapeDtypeStruct((2, rank, columns), jnp.float32),
        ),
        in_specs=[smem, smem, vmem, vmem, vmem],
        out_specs=(vmem, vmem),
        scratch_shapes=[
            pltpu.VMEM((half, padded, columns), jnp.bfloat16),
            pltpu.VMEM((half, padded, columns), jnp.bfloat16),
            pltpu.VMEM((chunks, half, padded, LANES), jnp.bfloat16),
            pltpu.VMEM((chunks, half, padded, LANES), jnp.bfloat16),
            pltpu.VMEM((half, 2, 1, padded), jnp.int32),
            pltpu.VMEM((half, 2, 1, padded), jnp.int32),
            pltpu.VMEM((half, rows, padded), jnp.bfloat16),
            pltpu.VMEM((chunks, rows, LANES), jnp.int16),
            pltpu.VMEM((chunks, rows, LANES), jnp.int16),
            pltpu.VMEM((chunks, scale_rows, LANES), jnp.float32),
            pltpu.VMEM((chunks, scale_rows, LANES), jnp.float32),
            pltpu.VMEM((2, LINE_CELLS, columns), jnp.bfloat16),
            pltpu.VMEM((rows, columns), jnp.float32),
            pltpu.VMEM((2, rank, columns), jnp.float32),
            dma((half,)), dma((half,)), dma((chunks, half)), dma((chunks, half)), dma((half,)), dma((half,)),
            dma((chunks,)), dma((chunks,)), dma((chunks,)), dma((chunks,)), dma((2,)), dma((2,)), dma, dma,
        ],
        compiler_params=pltpu.CompilerParams(
            collective_id=0, has_side_effects=True, vmem_limit_bytes=56 * 1024 * 1024
        ),
    )(inv, skel_leaf, child, maps, omega)
    picks = lax.dynamic_slice_in_dim(skel_upper, position // 2, 1, 0)[0]
    return pl.pallas_call(
        solve_kernel,
        out_shape=(
            jax.ShapeDtypeStruct((rows, rank), jnp.float32),
            jax.ShapeDtypeStruct((rank, rank), jnp.float32),
            jax.ShapeDtypeStruct((rows, rank), jnp.float32),
        ),
        in_specs=[smem, smem, vmem, vmem],
        out_specs=(vmem, vmem, vmem),
        scratch_shapes=[pltpu.VMEM((rank, columns), jnp.float32)],
        compiler_params=pltpu.CompilerParams(vmem_limit_bytes=32 * 1024 * 1024),
    )(picks, (position % 2).reshape(1), cross, pair.reshape(2 * rank, columns))


def solution(mesh):
    in_specs = (
        P(("group", "row"), None),
        P(("group", "row"), None),
        P(("group", "row")),
        P(("group", "row")),
        P("group", None),
    )
    out_specs = (P(("group", "row"), None), P(("group", "row"), None), P(("group", "row"), None))
    return jax.shard_map(local, mesh=mesh, in_specs=in_specs, out_specs=out_specs, check_vma=False)
```

```python
import functools

import jax
import jax.numpy as jnp
from jax import lax
from jax.experimental import pallas as pl
from jax.experimental.pallas import tpu as pltpu
from jax.sharding import PartitionSpec as P

LINE_CELLS = 400
LANES = 128
TILE = 320
GROUP = 64
PIVOTS = 4
MESH = pl.DeviceIdType.MESH
HIGHEST = lax.Precision.HIGHEST


def exact_dot(left, right):
    return jnp.dot(left, right, precision=HIGHEST, preferred_element_type=jnp.float32)


def dot_rows(left, right):
    return lax.dot_general(
        left, right, (((1,), (1,)), ((), ())), precision=HIGHEST, preferred_element_type=jnp.float32
    )


def front_kernel(
    n, inv_ref, skel_ref, child_hbm, map_ref, omega_hbm, cross_ref, pair_ref,
    child_ref, omega_ref, child_sem, omega_sem,
    own_rows, got_own, far_rows, got_far, send_maps, got_maps, hot, coded, got_coded, scales, got_scales,
    halo, sketch, chosen,
    own_send, own_recv, far_send, far_recv, map_send, map_recv,
    code_send, code_recv, scale_send, scale_recv, halo_send, halo_recv, pair_send, pair_recv,
):
    me = lax.axis_index("row")
    rows = sketch.shape[0]
    columns = sketch.shape[1]
    rank = chosen.shape[1]
    padded = child_ref.shape[1]
    half = n // 2
    base = me // half * half
    place = me % half
    mirror = (me + half) % n
    other = mirror // half * half
    parity = me % 2
    partner = me + 1 - 2 * parity
    chunks = columns // LANES

    child_copy = pltpu.make_async_copy(child_hbm, child_ref, child_sem)
    child_copy.start()
    omega_copy = pltpu.make_async_copy(omega_hbm, omega_ref, omega_sem)
    omega_copy.start()
    halo[...] = jnp.zeros_like(halo)
    scales[...] = jnp.zeros_like(scales)
    barrier = pltpu.get_barrier_semaphore()

    def greet(j, carry):
        pl.semaphore_signal(barrier, inc=1, device_id={"row": (me + j) % n}, device_id_type=MESH)
        return carry

    lax.fori_loop(1, n, greet, 0)
    pl.semaphore_wait(barrier, n - 1)

    def peer_copy(source, target, send, recv, j):
        return pltpu.make_async_remote_copy(
            source, target, send, recv,
            device_id={"row": base + (place + j) % half}, device_id_type=MESH,
        )

    def own_copy(j):
        return peer_copy(own_rows.at[j], got_own.at[j], own_send.at[j], own_recv.at[j], j)

    def far_copy(q, j):
        return peer_copy(far_rows.at[q, j], got_far.at[q, j], far_send.at[q, j], far_recv.at[q, j], j)

    def map_copy(j):
        return peer_copy(send_maps.at[j], got_maps.at[j], map_send.at[j], map_recv.at[j], j)

    def code_copy(q):
        return pltpu.make_async_remote_copy(
            coded.at[q], got_coded.at[q], code_send.at[q], code_recv.at[q],
            device_id={"row": mirror}, device_id_type=MESH,
        )

    def scale_copy(q):
        return pltpu.make_async_remote_copy(
            scales.at[q], got_scales.at[q], scale_send.at[q], scale_recv.at[q],
            device_id={"row": mirror}, device_id_type=MESH,
        )

    def halo_copy(side):
        start = rows - LINE_CELLS if side == 0 else 0
        return pltpu.make_async_remote_copy(
            omega_hbm.at[pl.ds(start, LINE_CELLS)], halo.at[side], halo_send.at[side], halo_recv.at[side],
            device_id={"row": (me + 1) % n if side == 0 else (me + n - 1) % n}, device_id_type=MESH,
        )

    def local_map(to):
        block = inv_ref[to]
        return jnp.where(block >= 0, map_ref[jnp.maximum(block, 0)] - to * rows, -1)

    def block_of(to):
        return jnp.maximum(inv_ref[to], 0)

    def send_map(j, carry):
        at = (place + j) % half
        send_maps[j, 0] = local_map(base + at)
        send_maps[j, 1] = local_map(other + at)
        map_copy(j).start()
        return carry

    def send_far(q):
        def step(j, carry):
            far_rows[q, j] = child_ref[block_of(other + (place + j) % half), :, q * LANES:(q + 1) * LANES]
            far_copy(q, j).start()
            return carry

        lax.fori_loop(1, half, step, 0)

    def send_own(j, carry):
        own_rows[j] = child_ref[block_of(base + (place + j) % half)]
        own_copy(j).start()
        return carry

    def send_group(g):
        low, high = 1 + (half - 1) * g // chunks, 1 + (half - 1) * (g + 1) // chunks
        lax.fori_loop(low, high, send_own, 0)

    lax.fori_loop(1, half, send_map, 0)
    child_copy.wait()
    send_far(0)

    @pl.when(me < n - 1)
    def _():
        halo_copy(0).start()

    @pl.when(me > 0)
    def _():
        halo_copy(1).start()

    for q in range(1, chunks):
        send_far(q)
    send_group(0)

    def mark(j, numbers):
        def step(t, carry):
            start = pl.multiple_of(t * TILE, 16)
            row = lax.broadcasted_iota(jnp.int32, (TILE, padded), 0) + start
            hot[j, pl.ds(start, TILE)] = (row == numbers).astype(jnp.float32).astype(jnp.bfloat16)
            return carry

        lax.fori_loop(0, rows // TILE, step, 0)

    mark(0, local_map(mirror))
    far_block = block_of(mirror)
    for q in range(chunks):
        got_far[q, 0] = child_ref[far_block, :, q * LANES:(q + 1) * LANES]

    def mark_peer(j, carry):
        map_copy(j).wait()
        mark(j, got_maps[j, 1])
        return carry

    lax.fori_loop(1, half, mark_peer, 0)

    eye = (
        lax.broadcasted_iota(jnp.int32, (GROUP, LANES), 0) == lax.broadcasted_iota(jnp.int32, (GROUP, LANES), 1)
    ).astype(jnp.float32)
    groups = TILE // GROUP

    for q in range(chunks):
        def arrived(j, carry):
            far_copy(q, j).wait()
            return carry

        lax.fori_loop(1, half, arrived, 0)

        def code(t, carry):
            start = pl.multiple_of(t * TILE, 16)

            def add(j, total):
                return total + jnp.dot(
                    hot[j, pl.ds(start, TILE)], got_far[q, j], preferred_element_type=jnp.float32
                )

            total = lax.fori_loop(0, half, add, jnp.zeros((TILE, LANES), jnp.float32))
            largest = jnp.max(jnp.abs(total), axis=1, keepdims=True)
            scale = largest * (1.0 / 32767.0)
            factor = jnp.where(largest > 0.0, 32767.0 / jnp.where(largest > 0.0, largest, 1.0), 0.0)
            whole = jnp.clip(jnp.floor(total * factor + 0.5), -32767.0, 32767.0)
            coded[q, pl.ds(start, TILE)] = whole.astype(jnp.int32).astype(jnp.int16)
            for u in range(groups):
                flat = jnp.sum(scale[u * GROUP:(u + 1) * GROUP] * eye, axis=0, keepdims=True)
                scales[q, pl.ds(t * groups + u, 1), :] = flat
            return carry

        lax.fori_loop(0, rows // TILE, code, 0)
        scale_copy(q).start()
        code_copy(q).start()
        if q + 1 < chunks:
            send_group(q + 1)

    @pl.when(me < n - 1)
    def _():
        halo_copy(0).wait_send()
        halo_copy(1).wait_recv()

    @pl.when(me > 0)
    def _():
        halo_copy(1).wait_send()
        halo_copy(0).wait_recv()

    omega_copy.wait()
    cell = lax.broadcasted_iota(jnp.int32, (LINE_CELLS, columns), 0)
    lines = rows // LINE_CELLS
    for line in range(lines):
        here = omega_ref[line * LINE_CELLS:(line + 1) * LINE_CELLS].astype(jnp.float32)
        above = halo[0] if line == 0 else omega_ref[(line - 1) * LINE_CELLS:line * LINE_CELLS]
        below = halo[1] if line == lines - 1 else omega_ref[(line + 1) * LINE_CELLS:(line + 2) * LINE_CELLS]
        left = jnp.where(cell == 0, 0.0, pltpu.roll(here, 1, 0))
        right = jnp.where(cell == LINE_CELLS - 1, 0.0, pltpu.roll(here, LINE_CELLS - 1, 0))
        sketch[line * LINE_CELLS:(line + 1) * LINE_CELLS] = (
            6.0 * here - above.astype(jnp.float32) - below.astype(jnp.float32) - left - right
        )

    mark(0, local_map(me))

    def mark_own(j, carry):
        mark(j, got_maps[j, 0])
        return carry

    lax.fori_loop(1, half, mark_own, 0)

    def extend_add(j, block):
        def step(t, carry):
            start = pl.multiple_of(t * TILE, 16)
            sketch[pl.ds(start, TILE)] += jnp.dot(
                hot[j, pl.ds(start, TILE)], block, preferred_element_type=jnp.float32
            )
            return carry

        lax.fori_loop(0, rows // TILE, step, 0)

    extend_add(0, child_ref[block_of(me)])

    def receive(j, carry):
        own_copy(j).wait()
        extend_add(j, got_own[j])
        return carry

    lax.fori_loop(1, half - half // 4, receive, 0)

    for q in range(chunks):
        if q == chunks // 2:
            lax.fori_loop(half - half // 4, half, receive, 0)
        scale_copy(q).wait()
        code_copy(q).wait()

        def decode(t, carry):
            for u in range(groups):
                start = pl.multiple_of(t * TILE + u * GROUP, 16)
                flat = got_scales[q, pl.ds(t * groups + u, 1), :]
                scale = jnp.sum(flat * eye, axis=1, keepdims=True)
                part = got_coded[q, pl.ds(start, GROUP)].astype(jnp.int32).astype(jnp.float32) * scale
                sketch[pl.ds(start, GROUP), q * LANES:(q + 1) * LANES] += part
            return carry

        lax.fori_loop(0, rows // TILE, decode, 0)

    def choose(i, carry):
        for u in range(8):
            chosen[parity, pl.ds(i * 8 + u, 1), :] = sketch[pl.ds(skel_ref[i * 8 + u], 1), :]
        return carry

    lax.fori_loop(0, rank // 8, choose, 0)
    pair_copy = pltpu.make_async_remote_copy(
        chosen.at[parity], chosen.at[parity], pair_send, pair_recv,
        device_id={"row": partner}, device_id_type=MESH,
    )
    pair_copy.start()
    own = chosen[parity]

    def cross(t, carry):
        start = pl.multiple_of(t * TILE, 16)
        cross_ref[pl.ds(start, TILE)] = dot_rows(sketch[pl.ds(start, TILE)], own)
        return carry

    lax.fori_loop(0, rows // TILE, cross, 0)
    pair_copy.wait()
    pair_ref[...] = chosen[...]


def invert_pair(first, second):
    size = first.shape[0]
    b = PIVOTS
    lane_id = lax.broadcasted_iota(jnp.int32, (size, size), 1)
    eight = lax.broadcasted_iota(jnp.int32, (8, size), 0)
    matrices = [first, second]
    for k in range(0, size, b):
        pivots = (lane_id >= k) & (lane_id < k + b)
        for m in range(2):
            a = matrices[m]
            columns = [jnp.broadcast_to(a[:, k + i:k + i + 1], (size, size)) for i in range(b)]
            small = [[columns[j][k + i:k + i + 1] for j in range(b)] for i in range(b)]
            rows = [jnp.where(pivots[:1], (lane_id[:1] == k + i).astype(jnp.float32), a[k + i:k + i + 1]) for i in range(b)]
            for p in range(b):
                scale = 1.0 / small[p][p]
                rows[p] = rows[p] * scale
                for j in range(p + 1, b):
                    small[p][j] = small[p][j] * scale
                for i in range(b):
                    if i != p:
                        rows[i] = rows[i] - small[i][p] * rows[p]
                        for j in range(p + 1, b):
                            small[i][j] = small[i][j] - small[i][p] * small[p][j]
            rest = jnp.where(pivots, 0.0, a)
            for i in range(b):
                rest = rest - columns[i] * rows[i]
            at = k // 8 * 8
            group = rest[at:at + 8]
            for i in range(b):
                group = jnp.where(eight == k + i - at, rows[i], group)
            matrices[m] = jnp.concatenate([x for x in (rest[:at], group, rest[at + 8:]) if x.shape[0]], axis=0)
    return matrices


def solve_kernel(pick_ref, side_ref, cross_hbm, pair_ref, leaf_ref, upper_ref, nested_ref, picked, cross_ref, cross_sem):
    rank = picked.shape[0]
    cross_copy = pltpu.make_async_copy(cross_hbm, cross_ref, cross_sem)
    cross_copy.start()
    own = pair_ref[pl.ds(pl.multiple_of(side_ref[0] * rank, rank), rank), :]

    def pick(i, carry):
        for u in range(8):
            picked[pl.ds(i * 8 + u, 1), :] = pair_ref[pl.ds(pick_ref[i * 8 + u], 1), :]
        return carry

    lax.fori_loop(0, rank // 8, pick, 0)
    upper_rows = picked[...]
    leaf_inverse, upper_inverse = invert_pair(dot_rows(own, own), dot_rows(upper_rows, upper_rows))
    upper = exact_dot(dot_rows(own, upper_rows), upper_inverse)
    upper_ref[...] = upper
    tile = LINE_CELLS

    cross_copy.wait()

    def finish(t, carry):
        start = pl.multiple_of(t * tile, 16)
        terms = cross_ref[pl.ds(start, tile)]
        leaf = exact_dot(terms, leaf_inverse)
        leaf_ref[pl.ds(start, tile)] = leaf
        nested_ref[pl.ds(start, tile)] = exact_dot(leaf, upper)
        return carry

    lax.fori_loop(0, cross_ref.shape[0] // tile, finish, 0)


def local(omega, child_sketch, child_map, skel_leaf, skel_upper):
    rows, columns = omega.shape
    rank = skel_leaf.shape[0]
    n = lax.axis_size("row")
    position = lax.axis_index("row")
    slot = 4 * rows // n
    blocks = child_sketch.shape[0] // slot
    padded = -(-slot // 16) * 16
    child = child_sketch.reshape(blocks, slot, columns)
    maps = child_map.reshape(blocks, 1, slot)
    targets = maps[:, 0, 0] // rows
    if padded != slot:
        child = jnp.pad(child, ((0, 0), (0, padded - slot), (0, 0)))
        maps = jnp.pad(maps, ((0, 0), (0, 0), (0, padded - slot)), constant_values=-1)
    numbers = jnp.arange(blocks, dtype=jnp.int32)
    places = jnp.arange(n, dtype=jnp.int32)
    inv = jnp.max(jnp.where(targets[None, :] == places[:, None], numbers[None, :], -1), axis=1)
    vmem = pl.BlockSpec(memory_space=pltpu.VMEM)
    smem = pl.BlockSpec(memory_space=pltpu.SMEM)
    anywhere = pl.BlockSpec(memory_space=pl.ANY)
    dma = pltpu.SemaphoreType.DMA
    half, chunks = n // 2, columns // LANES
    scale_rows = -(-rows // (GROUP * 8)) * 8
    cross, pair = pl.pallas_call(
        functools.partial(front_kernel, n),
        out_shape=(
            jax.ShapeDtypeStruct((rows, rank), jnp.float32),
            jax.ShapeDtypeStruct((2, rank, columns), jnp.float32),
        ),
        in_specs=[smem, smem, anywhere, vmem, anywhere],
        out_specs=(vmem, vmem),
        scratch_shapes=[
            pltpu.VMEM((blocks, padded, columns), jnp.bfloat16),
            pltpu.VMEM((rows, columns), jnp.bfloat16),
            dma, dma,
            pltpu.VMEM((half, padded, columns), jnp.bfloat16),
            pltpu.VMEM((half, padded, columns), jnp.bfloat16),
            pltpu.VMEM((chunks, half, padded, LANES), jnp.bfloat16),
            pltpu.VMEM((chunks, half, padded, LANES), jnp.bfloat16),
            pltpu.VMEM((half, 2, 1, padded), jnp.int32),
            pltpu.VMEM((half, 2, 1, padded), jnp.int32),
            pltpu.VMEM((half, rows, padded), jnp.bfloat16),
            pltpu.VMEM((chunks, rows, LANES), jnp.int16),
            pltpu.VMEM((chunks, rows, LANES), jnp.int16),
            pltpu.VMEM((chunks, scale_rows, LANES), jnp.float32),
            pltpu.VMEM((chunks, scale_rows, LANES), jnp.float32),
            pltpu.VMEM((2, LINE_CELLS, columns), jnp.bfloat16),
            pltpu.VMEM((rows, columns), jnp.float32),
            pltpu.VMEM((2, rank, columns), jnp.float32),
            dma((half,)), dma((half,)), dma((chunks, half)), dma((chunks, half)), dma((half,)), dma((half,)),
            dma((chunks,)), dma((chunks,)), dma((chunks,)), dma((chunks,)), dma((2,)), dma((2,)), dma, dma,
        ],
        compiler_params=pltpu.CompilerParams(
            collective_id=0, has_side_effects=True, vmem_limit_bytes=56 * 1024 * 1024
        ),
    )(inv, skel_leaf, child, maps, omega)
    picks = lax.dynamic_slice_in_dim(skel_upper, position // 2, 1, 0)[0]
    return pl.pallas_call(
        solve_kernel,
        out_shape=(
            jax.ShapeDtypeStruct((rows, rank), jnp.float32),
            jax.ShapeDtypeStruct((rank, rank), jnp.float32),
            jax.ShapeDtypeStruct((rows, rank), jnp.float32),
        ),
        in_specs=[smem, smem, anywhere, vmem],
        out_specs=(vmem, vmem, vmem),
        scratch_shapes=[pltpu.VMEM((rank, columns), jnp.float32), pltpu.VMEM((rows, rank), jnp.float32), dma],
        compiler_params=pltpu.CompilerParams(vmem_limit_bytes=56 * 1024 * 1024),
    )(picks, (position % 2).reshape(1), cross, pair.reshape(2 * rank, columns))


def solution(mesh):
    in_specs = (
        P(("group", "row"), None),
        P(("group", "row"), None),
        P(("group", "row")),
        P(("group", "row")),
        P("group", None),
    )
    out_specs = (P(("group", "row"), None), P(("group", "row"), None), P(("group", "row"), None))
    return jax.shard_map(local, mesh=mesh, in_specs=in_specs, out_specs=out_specs, check_vma=False)
```

```python
import functools

import jax
import jax.numpy as jnp
from jax import lax
from jax.experimental import pallas as pl
from jax.experimental.pallas import tpu as pltpu
from jax.sharding import PartitionSpec as P

LINE_CELLS = 400
LANES = 128
TILE = 320
GROUP = 64
PIVOTS = 4
MESH = pl.DeviceIdType.MESH
HIGHEST = lax.Precision.HIGHEST


def exact_dot(left, right):
    return jnp.dot(left, right, precision=HIGHEST, preferred_element_type=jnp.float32)


def dot_rows(left, right):
    return lax.dot_general(
        left, right, (((1,), (1,)), ((), ())), precision=HIGHEST, preferred_element_type=jnp.float32
    )


def front_kernel(
    n, number_ref, skel_ref, child_hbm, map_ref, omega_hbm, cross_ref, pair_ref,
    inv_ref, child_ref, omega_ref, child_sem, omega_sem,
    own_rows, got_own, far_rows, got_far, send_maps, got_maps, hot, coded, got_coded, scales, got_scales,
    halo, sketch, chosen,
    own_send, own_recv, far_send, far_recv, map_send, map_recv,
    code_send, code_recv, scale_send, scale_recv, halo_send, halo_recv, pair_send, pair_recv,
):
    me = lax.axis_index("row")
    rows = sketch.shape[0]
    columns = sketch.shape[1]
    rank = chosen.shape[1]
    padded = child_ref.shape[1]
    half = n // 2
    base = me // half * half
    place = me % half
    mirror = (me + half) % n
    other = mirror // half * half
    parity = me % 2
    partner = me + 1 - 2 * parity
    chunks = columns // LANES

    child_copy = pltpu.make_async_copy(child_hbm, child_ref, child_sem)
    child_copy.start()
    omega_copy = pltpu.make_async_copy(omega_hbm, omega_ref, omega_sem)
    omega_copy.start()
    halo[...] = jnp.zeros_like(halo)
    scales[...] = jnp.zeros_like(scales)
    barrier = pltpu.get_barrier_semaphore()

    def greet(j, carry):
        pl.semaphore_signal(barrier, inc=1, device_id={"row": (me + j) % n}, device_id_type=MESH)
        return carry

    lax.fori_loop(1, n, greet, 0)
    blocks = child_ref.shape[0]
    slot = number_ref.shape[0] // blocks

    def look_up(to, carry):
        found = jnp.int32(-1)
        for k in range(blocks):
            first = number_ref[k * slot]
            found = jnp.where((first >= to * rows) & (first < (to + 1) * rows), k, found)
        inv_ref[to] = found
        return carry

    lax.fori_loop(0, n, look_up, 0)
    pl.semaphore_wait(barrier, n - 1)

    def peer_copy(source, target, send, recv, j):
        return pltpu.make_async_remote_copy(
            source, target, send, recv,
            device_id={"row": base + (place + j) % half}, device_id_type=MESH,
        )

    def own_copy(j):
        return peer_copy(own_rows.at[j], got_own.at[j], own_send.at[j], own_recv.at[j], j)

    def far_copy(q, j):
        return peer_copy(far_rows.at[q, j], got_far.at[q, j], far_send.at[q, j], far_recv.at[q, j], j)

    def map_copy(j):
        return peer_copy(send_maps.at[j], got_maps.at[j], map_send.at[j], map_recv.at[j], j)

    def code_copy(q):
        return pltpu.make_async_remote_copy(
            coded.at[q], got_coded.at[q], code_send.at[q], code_recv.at[q],
            device_id={"row": mirror}, device_id_type=MESH,
        )

    def scale_copy(q):
        return pltpu.make_async_remote_copy(
            scales.at[q], got_scales.at[q], scale_send.at[q], scale_recv.at[q],
            device_id={"row": mirror}, device_id_type=MESH,
        )

    def halo_copy(side):
        start = rows - LINE_CELLS if side == 0 else 0
        return pltpu.make_async_remote_copy(
            omega_hbm.at[pl.ds(start, LINE_CELLS)], halo.at[side], halo_send.at[side], halo_recv.at[side],
            device_id={"row": (me + 1) % n if side == 0 else (me + n - 1) % n}, device_id_type=MESH,
        )

    def local_map(to):
        block = inv_ref[to]
        return jnp.where(block >= 0, map_ref[jnp.maximum(block, 0)] - to * rows, -1)

    def block_of(to):
        return jnp.maximum(inv_ref[to], 0)

    def send_map(j, carry):
        at = (place + j) % half
        send_maps[j, 0] = local_map(base + at)
        send_maps[j, 1] = local_map(other + at)
        map_copy(j).start()
        return carry

    def send_far(q):
        def step(j, carry):
            far_rows[q, j] = child_ref[block_of(other + (place + j) % half), :, q * LANES:(q + 1) * LANES]
            far_copy(q, j).start()
            return carry

        lax.fori_loop(1, half, step, 0)

    def send_own(j, carry):
        own_rows[j] = child_ref[block_of(base + (place + j) % half)]
        own_copy(j).start()
        return carry

    def send_group(g):
        low, high = 1 + (half - 1) * g // chunks, 1 + (half - 1) * (g + 1) // chunks
        lax.fori_loop(low, high, send_own, 0)

    lax.fori_loop(1, half, send_map, 0)
    child_copy.wait()
    send_far(0)

    @pl.when(me < n - 1)
    def _():
        halo_copy(0).start()

    @pl.when(me > 0)
    def _():
        halo_copy(1).start()

    for q in range(1, chunks):
        send_far(q)
    send_group(0)

    def mark(j, numbers):
        def step(t, carry):
            start = pl.multiple_of(t * TILE, 16)
            row = lax.broadcasted_iota(jnp.int32, (TILE, padded), 0) + start
            hot[j, pl.ds(start, TILE)] = (row == numbers).astype(jnp.float32).astype(jnp.bfloat16)
            return carry

        lax.fori_loop(0, rows // TILE, step, 0)

    mark(0, local_map(mirror))
    far_block = block_of(mirror)
    for q in range(chunks):
        got_far[q, 0] = child_ref[far_block, :, q * LANES:(q + 1) * LANES]

    def mark_peer(j, carry):
        map_copy(j).wait()
        mark(j, got_maps[j, 1])
        return carry

    lax.fori_loop(1, half, mark_peer, 0)

    eye = (
        lax.broadcasted_iota(jnp.int32, (GROUP, LANES), 0) == lax.broadcasted_iota(jnp.int32, (GROUP, LANES), 1)
    ).astype(jnp.float32)
    groups = TILE // GROUP

    for q in range(chunks):
        def arrived(j, carry):
            far_copy(q, j).wait()
            return carry

        lax.fori_loop(1, half, arrived, 0)

        def code(t, carry):
            start = pl.multiple_of(t * TILE, 16)

            def add(j, total):
                return total + jnp.dot(
                    hot[j, pl.ds(start, TILE)], got_far[q, j], preferred_element_type=jnp.float32
                )

            total = lax.fori_loop(0, half, add, jnp.zeros((TILE, LANES), jnp.float32))
            largest = jnp.max(jnp.abs(total), axis=1, keepdims=True)
            scale = largest * (1.0 / 32767.0)
            factor = jnp.where(largest > 0.0, 32767.0 / jnp.where(largest > 0.0, largest, 1.0), 0.0)
            whole = jnp.clip(jnp.floor(total * factor + 0.5), -32767.0, 32767.0)
            coded[q, pl.ds(start, TILE)] = whole.astype(jnp.int32).astype(jnp.int16)
            for u in range(groups):
                flat = jnp.sum(scale[u * GROUP:(u + 1) * GROUP] * eye, axis=0, keepdims=True)
                scales[q, pl.ds(t * groups + u, 1), :] = flat
            return carry

        lax.fori_loop(0, rows // TILE, code, 0)
        scale_copy(q).start()
        code_copy(q).start()
        if q + 1 < chunks:
            send_group(q + 1)

    @pl.when(me < n - 1)
    def _():
        halo_copy(0).wait_send()
        halo_copy(1).wait_recv()

    @pl.when(me > 0)
    def _():
        halo_copy(1).wait_send()
        halo_copy(0).wait_recv()

    omega_copy.wait()
    cell = lax.broadcasted_iota(jnp.int32, (LINE_CELLS, columns), 0)
    lines = rows // LINE_CELLS
    for line in range(lines):
        here = omega_ref[line * LINE_CELLS:(line + 1) * LINE_CELLS].astype(jnp.float32)
        above = halo[0] if line == 0 else omega_ref[(line - 1) * LINE_CELLS:line * LINE_CELLS]
        below = halo[1] if line == lines - 1 else omega_ref[(line + 1) * LINE_CELLS:(line + 2) * LINE_CELLS]
        left = jnp.where(cell == 0, 0.0, pltpu.roll(here, 1, 0))
        right = jnp.where(cell == LINE_CELLS - 1, 0.0, pltpu.roll(here, LINE_CELLS - 1, 0))
        sketch[line * LINE_CELLS:(line + 1) * LINE_CELLS] = (
            6.0 * here - above.astype(jnp.float32) - below.astype(jnp.float32) - left - right
        )

    mark(0, local_map(me))

    def mark_own(j, carry):
        mark(j, got_maps[j, 0])
        return carry

    lax.fori_loop(1, half, mark_own, 0)

    def extend_add(j, block):
        def step(t, carry):
            start = pl.multiple_of(t * TILE, 16)
            sketch[pl.ds(start, TILE)] += jnp.dot(
                hot[j, pl.ds(start, TILE)], block, preferred_element_type=jnp.float32
            )
            return carry

        lax.fori_loop(0, rows // TILE, step, 0)

    extend_add(0, child_ref[block_of(me)])

    def receive(j, carry):
        own_copy(j).wait()
        extend_add(j, got_own[j])
        return carry

    lax.fori_loop(1, half - half // 4, receive, 0)

    for q in range(chunks):
        if q == chunks // 2:
            lax.fori_loop(half - half // 4, half, receive, 0)
        scale_copy(q).wait()
        code_copy(q).wait()

        def decode(t, carry):
            for u in range(groups):
                start = pl.multiple_of(t * TILE + u * GROUP, 16)
                flat = got_scales[q, pl.ds(t * groups + u, 1), :]
                scale = jnp.sum(flat * eye, axis=1, keepdims=True)
                part = got_coded[q, pl.ds(start, GROUP)].astype(jnp.int32).astype(jnp.float32) * scale
                sketch[pl.ds(start, GROUP), q * LANES:(q + 1) * LANES] += part
            return carry

        lax.fori_loop(0, rows // TILE, decode, 0)

    def choose(i, carry):
        for u in range(8):
            chosen[parity, pl.ds(i * 8 + u, 1), :] = sketch[pl.ds(skel_ref[i * 8 + u], 1), :]
        return carry

    lax.fori_loop(0, rank // 8, choose, 0)
    pair_copy = pltpu.make_async_remote_copy(
        chosen.at[parity], chosen.at[parity], pair_send, pair_recv,
        device_id={"row": partner}, device_id_type=MESH,
    )
    pair_copy.start()
    own = chosen[parity]

    def cross(t, carry):
        start = pl.multiple_of(t * TILE, 16)
        cross_ref[pl.ds(start, TILE)] = dot_rows(sketch[pl.ds(start, TILE)], own)
        return carry

    lax.fori_loop(0, rows // TILE, cross, 0)
    pair_copy.wait()
    pair_ref[...] = chosen[...]


def invert_pair(first, second):
    size = first.shape[0]
    b = PIVOTS
    lane_id = lax.broadcasted_iota(jnp.int32, (size, size), 1)
    eight = lax.broadcasted_iota(jnp.int32, (8, size), 0)
    matrices = [first, second]
    for k in range(0, size, b):
        pivots = (lane_id >= k) & (lane_id < k + b)
        for m in range(2):
            a = matrices[m]
            columns = [jnp.broadcast_to(a[:, k + i:k + i + 1], (size, size)) for i in range(b)]
            small = [[columns[j][k + i:k + i + 1] for j in range(b)] for i in range(b)]
            rows = [jnp.where(pivots[:1], (lane_id[:1] == k + i).astype(jnp.float32), a[k + i:k + i + 1]) for i in range(b)]
            for p in range(b):
                scale = 1.0 / small[p][p]
                rows[p] = rows[p] * scale
                for j in range(p + 1, b):
                    small[p][j] = small[p][j] * scale
                for i in range(b):
                    if i != p:
                        rows[i] = rows[i] - small[i][p] * rows[p]
                        for j in range(p + 1, b):
                            small[i][j] = small[i][j] - small[i][p] * small[p][j]
            rest = jnp.where(pivots, 0.0, a)
            for i in range(b):
                rest = rest - columns[i] * rows[i]
            at = k // 8 * 8
            group = rest[at:at + 8]
            for i in range(b):
                group = jnp.where(eight == k + i - at, rows[i], group)
            matrices[m] = jnp.concatenate([x for x in (rest[:at], group, rest[at + 8:]) if x.shape[0]], axis=0)
    return matrices


def solve_kernel(pick_ref, cross_hbm, pair_ref, leaf_ref, upper_ref, nested_ref, picked, cross_ref, cross_sem):
    rank = picked.shape[0]
    cross_copy = pltpu.make_async_copy(cross_hbm, cross_ref, cross_sem)
    cross_copy.start()
    me = lax.axis_index("row")
    own = pair_ref[pl.ds(pl.multiple_of(me % 2 * rank, rank), rank), :]

    def pick(i, carry):
        for u in range(8):
            picked[pl.ds(i * 8 + u, 1), :] = pair_ref[pl.ds(pick_ref[me // 2, i * 8 + u], 1), :]
        return carry

    lax.fori_loop(0, rank // 8, pick, 0)
    upper_rows = picked[...]
    leaf_inverse, upper_inverse = invert_pair(dot_rows(own, own), dot_rows(upper_rows, upper_rows))
    upper = exact_dot(dot_rows(own, upper_rows), upper_inverse)
    upper_ref[...] = upper
    tile = LINE_CELLS

    cross_copy.wait()

    def finish(t, carry):
        start = pl.multiple_of(t * tile, 16)
        terms = cross_ref[pl.ds(start, tile)]
        leaf = exact_dot(terms, leaf_inverse)
        leaf_ref[pl.ds(start, tile)] = leaf
        nested_ref[pl.ds(start, tile)] = exact_dot(leaf, upper)
        return carry

    lax.fori_loop(0, cross_ref.shape[0] // tile, finish, 0)


def local(omega, child_sketch, child_map, skel_leaf, skel_upper):
    rows, columns = omega.shape
    rank = skel_leaf.shape[0]
    n = lax.axis_size("row")
    slot = 4 * rows // n
    blocks = child_sketch.shape[0] // slot
    padded = -(-slot // 16) * 16
    child = child_sketch.reshape(blocks, slot, columns)
    maps = child_map.reshape(blocks, 1, slot)
    if padded != slot:
        child = jnp.pad(child, ((0, 0), (0, padded - slot), (0, 0)))
        maps = jnp.pad(maps, ((0, 0), (0, 0), (0, padded - slot)), constant_values=-1)
    vmem = pl.BlockSpec(memory_space=pltpu.VMEM)
    smem = pl.BlockSpec(memory_space=pltpu.SMEM)
    anywhere = pl.BlockSpec(memory_space=pl.ANY)
    dma = pltpu.SemaphoreType.DMA
    half, chunks = n // 2, columns // LANES
    scale_rows = -(-rows // (GROUP * 8)) * 8
    cross, pair = pl.pallas_call(
        functools.partial(front_kernel, n),
        out_shape=(
            jax.ShapeDtypeStruct((rows, rank), jnp.float32),
            jax.ShapeDtypeStruct((2, rank, columns), jnp.float32),
        ),
        in_specs=[smem, smem, anywhere, vmem, anywhere],
        out_specs=(vmem, vmem),
        scratch_shapes=[
            pltpu.SMEM((n,), jnp.int32),
            pltpu.VMEM((blocks, padded, columns), jnp.bfloat16),
            pltpu.VMEM((rows, columns), jnp.bfloat16),
            dma, dma,
            pltpu.VMEM((half, padded, columns), jnp.bfloat16),
            pltpu.VMEM((half, padded, columns), jnp.bfloat16),
            pltpu.VMEM((chunks, half, padded, LANES), jnp.bfloat16),
            pltpu.VMEM((chunks, half, padded, LANES), jnp.bfloat16),
            pltpu.VMEM((half, 2, 1, padded), jnp.int32),
            pltpu.VMEM((half, 2, 1, padded), jnp.int32),
            pltpu.VMEM((half, rows, padded), jnp.bfloat16),
            pltpu.VMEM((chunks, rows, LANES), jnp.int16),
            pltpu.VMEM((chunks, rows, LANES), jnp.int16),
            pltpu.VMEM((chunks, scale_rows, LANES), jnp.float32),
            pltpu.VMEM((chunks, scale_rows, LANES), jnp.float32),
            pltpu.VMEM((2, LINE_CELLS, columns), jnp.bfloat16),
            pltpu.VMEM((rows, columns), jnp.float32),
            pltpu.VMEM((2, rank, columns), jnp.float32),
            dma((half,)), dma((half,)), dma((chunks, half)), dma((chunks, half)), dma((half,)), dma((half,)),
            dma((chunks,)), dma((chunks,)), dma((chunks,)), dma((chunks,)), dma((2,)), dma((2,)), dma, dma,
        ],
        compiler_params=pltpu.CompilerParams(
            collective_id=0, has_side_effects=True, vmem_limit_bytes=56 * 1024 * 1024
        ),
    )(child_map, skel_leaf, child, maps, omega)
    return pl.pallas_call(
        solve_kernel,
        out_shape=(
            jax.ShapeDtypeStruct((rows, rank), jnp.float32),
            jax.ShapeDtypeStruct((rank, rank), jnp.float32),
            jax.ShapeDtypeStruct((rows, rank), jnp.float32),
        ),
        in_specs=[smem, anywhere, vmem],
        out_specs=(vmem, vmem, vmem),
        scratch_shapes=[pltpu.VMEM((rank, columns), jnp.float32), pltpu.VMEM((rows, rank), jnp.float32), dma],
        compiler_params=pltpu.CompilerParams(vmem_limit_bytes=56 * 1024 * 1024),
    )(skel_upper, cross, pair.reshape(2 * rank, columns))


def solution(mesh):
    in_specs = (
        P(("group", "row"), None),
        P(("group", "row"), None),
        P(("group", "row")),
        P(("group", "row")),
        P("group", None),
    )
    out_specs = (P(("group", "row"), None), P(("group", "row"), None), P(("group", "row"), None))
    return jax.shard_map(local, mesh=mesh, in_specs=in_specs, out_specs=out_specs, check_vma=False)
```

```python
import functools

import jax
import jax.numpy as jnp
from jax import lax
from jax.experimental import pallas as pl
from jax.experimental.pallas import tpu as pltpu
from jax.sharding import PartitionSpec as P

LINE_CELLS = 400
LANES = 128
TILE = 320
GROUP = 64
PIVOTS = 4
MESH = pl.DeviceIdType.MESH
HIGHEST = lax.Precision.HIGHEST


def exact_dot(left, right):
    return jnp.dot(left, right, precision=HIGHEST, preferred_element_type=jnp.float32)


def dot_rows(left, right):
    return lax.dot_general(
        left, right, (((1,), (1,)), ((), ())), precision=HIGHEST, preferred_element_type=jnp.float32
    )


def front_kernel(
    n, number_ref, skel_ref, child_hbm, map_ref, omega_hbm, cross_ref, pair_ref,
    inv_ref, child_ref, omega_ref, child_sem, omega_sem,
    own_rows, got_own, far_rows, got_far, send_maps, got_maps, hot, coded, got_coded, scales, got_scales,
    halo, sketch, chosen,
    own_send, own_recv, far_send, far_recv, map_send, map_recv,
    code_send, code_recv, scale_send, scale_recv, halo_send, halo_recv, pair_send, pair_recv,
):
    me = lax.axis_index("row")
    rows = sketch.shape[0]
    columns = sketch.shape[1]
    rank = chosen.shape[1]
    padded = child_ref.shape[1]
    half = n // 2
    base = me // half * half
    place = me % half
    mirror = (me + half) % n
    other = mirror // half * half
    parity = me % 2
    partner = me + 1 - 2 * parity
    chunks = columns // LANES

    child_copy = pltpu.make_async_copy(child_hbm, child_ref, child_sem)
    child_copy.start()
    omega_copy = pltpu.make_async_copy(omega_hbm, omega_ref, omega_sem)
    omega_copy.start()
    halo[...] = jnp.zeros_like(halo)
    scales[...] = jnp.zeros_like(scales)
    barrier = pltpu.get_barrier_semaphore()

    def greet(j, carry):
        pl.semaphore_signal(barrier, inc=1, device_id={"row": (me + j) % n}, device_id_type=MESH)
        return carry

    lax.fori_loop(1, n, greet, 0)
    blocks = child_ref.shape[0]
    slot = number_ref.shape[0] // blocks

    def look_up(to, carry):
        found = jnp.int32(-1)
        for k in range(blocks):
            first = number_ref[k * slot]
            found = jnp.where((first >= to * rows) & (first < (to + 1) * rows), k, found)
        inv_ref[to] = found
        return carry

    lax.fori_loop(0, n, look_up, 0)
    pl.semaphore_wait(barrier, n - 1)

    def peer_copy(source, target, send, recv, j):
        return pltpu.make_async_remote_copy(
            source, target, send, recv,
            device_id={"row": base + (place + j) % half}, device_id_type=MESH,
        )

    def own_copy(j):
        return peer_copy(own_rows.at[j], got_own.at[j], own_send.at[j], own_recv.at[j], j)

    def far_copy(q, j):
        return peer_copy(far_rows.at[q, j], got_far.at[q, j], far_send.at[q, j], far_recv.at[q, j], j)

    def map_copy(j):
        return peer_copy(send_maps.at[j], got_maps.at[j], map_send.at[j], map_recv.at[j], j)

    def code_copy(q):
        return pltpu.make_async_remote_copy(
            coded.at[q], got_coded.at[q], code_send.at[q], code_recv.at[q],
            device_id={"row": mirror}, device_id_type=MESH,
        )

    def scale_copy(q):
        return pltpu.make_async_remote_copy(
            scales.at[q], got_scales.at[q], scale_send.at[q], scale_recv.at[q],
            device_id={"row": mirror}, device_id_type=MESH,
        )

    def halo_copy(side):
        start = rows - LINE_CELLS if side == 0 else 0
        return pltpu.make_async_remote_copy(
            omega_hbm.at[pl.ds(start, LINE_CELLS)], halo.at[side], halo_send.at[side], halo_recv.at[side],
            device_id={"row": (me + 1) % n if side == 0 else (me + n - 1) % n}, device_id_type=MESH,
        )

    def local_map(to):
        block = inv_ref[to]
        return jnp.where(block >= 0, map_ref[jnp.maximum(block, 0)] - to * rows, -1)

    def block_of(to):
        return jnp.maximum(inv_ref[to], 0)

    def send_map(j, carry):
        at = (place + j) % half
        send_maps[j, 0] = local_map(base + at)
        send_maps[j, 1] = local_map(other + at)
        map_copy(j).start()
        return carry

    def send_far(q):
        def step(j, carry):
            far_rows[q, j] = child_ref[block_of(other + (place + j) % half), :, q * LANES:(q + 1) * LANES]
            far_copy(q, j).start()
            return carry

        lax.fori_loop(1, half, step, 0)

    def send_own(j, carry):
        own_rows[j] = child_ref[block_of(base + (place + j) % half)]
        own_copy(j).start()
        return carry

    def send_group(g):
        low, high = 1 + (half - 1) * g // chunks, 1 + (half - 1) * (g + 1) // chunks
        lax.fori_loop(low, high, send_own, 0)

    lax.fori_loop(1, half, send_map, 0)
    child_copy.wait()
    send_far(0)

    @pl.when(me < n - 1)
    def _():
        halo_copy(0).start()

    @pl.when(me > 0)
    def _():
        halo_copy(1).start()

    for q in range(1, chunks):
        send_far(q)
    send_group(0)

    def mark(j, numbers):
        def step(t, carry):
            start = pl.multiple_of(t * TILE, 16)
            row = lax.broadcasted_iota(jnp.int32, (TILE, padded), 0) + start
            hot[j, pl.ds(start, TILE)] = (row == numbers).astype(jnp.float32).astype(jnp.bfloat16)
            return carry

        lax.fori_loop(0, rows // TILE, step, 0)

    mark(0, local_map(mirror))
    far_block = block_of(mirror)
    for q in range(chunks):
        got_far[q, 0] = child_ref[far_block, :, q * LANES:(q + 1) * LANES]

    def mark_peer(j, carry):
        map_copy(j).wait()
        mark(j, got_maps[j, 1])
        return carry

    lax.fori_loop(1, half, mark_peer, 0)

    eye = (
        lax.broadcasted_iota(jnp.int32, (GROUP, LANES), 0) == lax.broadcasted_iota(jnp.int32, (GROUP, LANES), 1)
    ).astype(jnp.float32)
    groups = TILE // GROUP

    for q in range(chunks):
        def arrived(j, carry):
            far_copy(q, j).wait()
            return carry

        lax.fori_loop(1, half, arrived, 0)

        def code(t, carry):
            start = pl.multiple_of(t * TILE, 16)

            def add(j, total):
                return total + jnp.dot(
                    hot[j, pl.ds(start, TILE)], got_far[q, j], preferred_element_type=jnp.float32
                )

            total = lax.fori_loop(0, half, add, jnp.zeros((TILE, LANES), jnp.float32))
            largest = jnp.max(jnp.abs(total), axis=1, keepdims=True)
            scale = largest * (1.0 / 32767.0)
            factor = jnp.where(largest > 0.0, 32767.0 / jnp.where(largest > 0.0, largest, 1.0), 0.0)
            whole = jnp.clip(jnp.floor(total * factor + 0.5), -32767.0, 32767.0)
            coded[q, pl.ds(start, TILE)] = whole.astype(jnp.int32).astype(jnp.int16)
            for u in range(groups):
                flat = jnp.sum(scale[u * GROUP:(u + 1) * GROUP] * eye, axis=0, keepdims=True)
                scales[q, pl.ds(t * groups + u, 1), :] = flat
            return carry

        lax.fori_loop(0, rows // TILE, code, 0)
        scale_copy(q).start()
        code_copy(q).start()
        if q + 1 < chunks:
            send_group(q + 1)

    @pl.when(me < n - 1)
    def _():
        halo_copy(0).wait_send()
        halo_copy(1).wait_recv()

    @pl.when(me > 0)
    def _():
        halo_copy(1).wait_send()
        halo_copy(0).wait_recv()

    omega_copy.wait()
    cell = lax.broadcasted_iota(jnp.int32, (LINE_CELLS, columns), 0)
    lines = rows // LINE_CELLS
    for line in range(lines):
        here = omega_ref[line * LINE_CELLS:(line + 1) * LINE_CELLS].astype(jnp.float32)
        above = halo[0] if line == 0 else omega_ref[(line - 1) * LINE_CELLS:line * LINE_CELLS]
        below = halo[1] if line == lines - 1 else omega_ref[(line + 1) * LINE_CELLS:(line + 2) * LINE_CELLS]
        left = jnp.where(cell == 0, 0.0, pltpu.roll(here, 1, 0))
        right = jnp.where(cell == LINE_CELLS - 1, 0.0, pltpu.roll(here, LINE_CELLS - 1, 0))
        sketch[line * LINE_CELLS:(line + 1) * LINE_CELLS] = (
            6.0 * here - above.astype(jnp.float32) - below.astype(jnp.float32) - left - right
        )

    mark(0, local_map(me))

    def mark_own(j, carry):
        mark(j, got_maps[j, 0])
        return carry

    lax.fori_loop(1, half, mark_own, 0)

    def extend_add(j, block):
        def step(t, carry):
            start = pl.multiple_of(t * TILE, 16)
            sketch[pl.ds(start, TILE)] += jnp.dot(
                hot[j, pl.ds(start, TILE)], block, preferred_element_type=jnp.float32
            )
            return carry

        lax.fori_loop(0, rows // TILE, step, 0)

    extend_add(0, child_ref[block_of(me)])

    def receive(j, carry):
        own_copy(j).wait()
        extend_add(j, got_own[j])
        return carry

    lax.fori_loop(1, half - half // 4, receive, 0)

    for q in range(chunks):
        if q == chunks - 1:
            lax.fori_loop(half - half // 4, half, receive, 0)
        scale_copy(q).wait()
        code_copy(q).wait()

        def decode(t, carry):
            for u in range(groups):
                start = pl.multiple_of(t * TILE + u * GROUP, 16)
                flat = got_scales[q, pl.ds(t * groups + u, 1), :]
                scale = jnp.sum(flat * eye, axis=1, keepdims=True)
                part = got_coded[q, pl.ds(start, GROUP)].astype(jnp.int32).astype(jnp.float32) * scale
                sketch[pl.ds(start, GROUP), q * LANES:(q + 1) * LANES] += part
            return carry

        lax.fori_loop(0, rows // TILE, decode, 0)

    def choose(i, carry):
        for u in range(8):
            chosen[parity, pl.ds(i * 8 + u, 1), :] = sketch[pl.ds(skel_ref[i * 8 + u], 1), :]
        return carry

    lax.fori_loop(0, rank // 8, choose, 0)
    pair_copy = pltpu.make_async_remote_copy(
        chosen.at[parity], chosen.at[parity], pair_send, pair_recv,
        device_id={"row": partner}, device_id_type=MESH,
    )
    pair_copy.start()
    own = chosen[parity]

    def cross(t, carry):
        start = pl.multiple_of(t * TILE, 16)
        cross_ref[pl.ds(start, TILE)] = dot_rows(sketch[pl.ds(start, TILE)], own)
        return carry

    lax.fori_loop(0, rows // TILE, cross, 0)
    pair_copy.wait()
    pair_ref[...] = chosen[...]


def invert_pair(first, second):
    size = first.shape[0]
    b = PIVOTS
    lane_id = lax.broadcasted_iota(jnp.int32, (size, size), 1)
    eight = lax.broadcasted_iota(jnp.int32, (8, size), 0)
    matrices = [first, second]
    for k in range(0, size, b):
        pivots = (lane_id >= k) & (lane_id < k + b)
        for m in range(2):
            a = matrices[m]
            columns = [jnp.broadcast_to(a[:, k + i:k + i + 1], (size, size)) for i in range(b)]
            small = [[columns[j][k + i:k + i + 1] for j in range(b)] for i in range(b)]
            rows = [jnp.where(pivots[:1], (lane_id[:1] == k + i).astype(jnp.float32), a[k + i:k + i + 1]) for i in range(b)]
            for p in range(b):
                scale = 1.0 / small[p][p]
                rows[p] = rows[p] * scale
                for j in range(p + 1, b):
                    small[p][j] = small[p][j] * scale
                for i in range(b):
                    if i != p:
                        rows[i] = rows[i] - small[i][p] * rows[p]
                        for j in range(p + 1, b):
                            small[i][j] = small[i][j] - small[i][p] * small[p][j]
            rest = jnp.where(pivots, 0.0, a)
            for i in range(b):
                rest = rest - columns[i] * rows[i]
            at = k // 8 * 8
            group = rest[at:at + 8]
            for i in range(b):
                group = jnp.where(eight == k + i - at, rows[i], group)
            matrices[m] = jnp.concatenate([x for x in (rest[:at], group, rest[at + 8:]) if x.shape[0]], axis=0)
    return matrices


def solve_kernel(pick_ref, cross_hbm, pair_ref, leaf_ref, upper_ref, nested_ref, picked, cross_ref, cross_sem):
    rank = picked.shape[0]
    cross_copy = pltpu.make_async_copy(cross_hbm, cross_ref, cross_sem)
    cross_copy.start()
    me = lax.axis_index("row")
    own = pair_ref[pl.ds(pl.multiple_of(me % 2 * rank, rank), rank), :]

    def pick(i, carry):
        for u in range(8):
            picked[pl.ds(i * 8 + u, 1), :] = pair_ref[pl.ds(pick_ref[me // 2, i * 8 + u], 1), :]
        return carry

    lax.fori_loop(0, rank // 8, pick, 0)
    upper_rows = picked[...]
    leaf_inverse, upper_inverse = invert_pair(dot_rows(own, own), dot_rows(upper_rows, upper_rows))
    upper = exact_dot(dot_rows(own, upper_rows), upper_inverse)
    upper_ref[...] = upper
    tile = LINE_CELLS

    cross_copy.wait()

    def finish(t, carry):
        start = pl.multiple_of(t * tile, 16)
        terms = cross_ref[pl.ds(start, tile)]
        leaf = exact_dot(terms, leaf_inverse)
        leaf_ref[pl.ds(start, tile)] = leaf
        nested_ref[pl.ds(start, tile)] = exact_dot(leaf, upper)
        return carry

    lax.fori_loop(0, cross_ref.shape[0] // tile, finish, 0)


def local(omega, child_sketch, child_map, skel_leaf, skel_upper):
    rows, columns = omega.shape
    rank = skel_leaf.shape[0]
    n = lax.axis_size("row")
    slot = 4 * rows // n
    blocks = child_sketch.shape[0] // slot
    padded = -(-slot // 16) * 16
    child = child_sketch.reshape(blocks, slot, columns)
    maps = child_map.reshape(blocks, 1, slot)
    if padded != slot:
        child = jnp.pad(child, ((0, 0), (0, padded - slot), (0, 0)))
        maps = jnp.pad(maps, ((0, 0), (0, 0), (0, padded - slot)), constant_values=-1)
    vmem = pl.BlockSpec(memory_space=pltpu.VMEM)
    smem = pl.BlockSpec(memory_space=pltpu.SMEM)
    anywhere = pl.BlockSpec(memory_space=pl.ANY)
    dma = pltpu.SemaphoreType.DMA
    half, chunks = n // 2, columns // LANES
    scale_rows = -(-rows // (GROUP * 8)) * 8
    cross, pair = pl.pallas_call(
        functools.partial(front_kernel, n),
        out_shape=(
            jax.ShapeDtypeStruct((rows, rank), jnp.float32),
            jax.ShapeDtypeStruct((2, rank, columns), jnp.float32),
        ),
        in_specs=[smem, smem, anywhere, vmem, anywhere],
        out_specs=(vmem, vmem),
        scratch_shapes=[
            pltpu.SMEM((n,), jnp.int32),
            pltpu.VMEM((blocks, padded, columns), jnp.bfloat16),
            pltpu.VMEM((rows, columns), jnp.bfloat16),
            dma, dma,
            pltpu.VMEM((half, padded, columns), jnp.bfloat16),
            pltpu.VMEM((half, padded, columns), jnp.bfloat16),
            pltpu.VMEM((chunks, half, padded, LANES), jnp.bfloat16),
            pltpu.VMEM((chunks, half, padded, LANES), jnp.bfloat16),
            pltpu.VMEM((half, 2, 1, padded), jnp.int32),
            pltpu.VMEM((half, 2, 1, padded), jnp.int32),
            pltpu.VMEM((half, rows, padded), jnp.bfloat16),
            pltpu.VMEM((chunks, rows, LANES), jnp.int16),
            pltpu.VMEM((chunks, rows, LANES), jnp.int16),
            pltpu.VMEM((chunks, scale_rows, LANES), jnp.float32),
            pltpu.VMEM((chunks, scale_rows, LANES), jnp.float32),
            pltpu.VMEM((2, LINE_CELLS, columns), jnp.bfloat16),
            pltpu.VMEM((rows, columns), jnp.float32),
            pltpu.VMEM((2, rank, columns), jnp.float32),
            dma((half,)), dma((half,)), dma((chunks, half)), dma((chunks, half)), dma((half,)), dma((half,)),
            dma((chunks,)), dma((chunks,)), dma((chunks,)), dma((chunks,)), dma((2,)), dma((2,)), dma, dma,
        ],
        compiler_params=pltpu.CompilerParams(
            collective_id=0, has_side_effects=True, vmem_limit_bytes=56 * 1024 * 1024
        ),
    )(child_map, skel_leaf, child, maps, omega)
    return pl.pallas_call(
        solve_kernel,
        out_shape=(
            jax.ShapeDtypeStruct((rows, rank), jnp.float32),
            jax.ShapeDtypeStruct((rank, rank), jnp.float32),
            jax.ShapeDtypeStruct((rows, rank), jnp.float32),
        ),
        in_specs=[smem, anywhere, vmem],
        out_specs=(vmem, vmem, vmem),
        scratch_shapes=[pltpu.VMEM((rank, columns), jnp.float32), pltpu.VMEM((rows, rank), jnp.float32), dma],
        compiler_params=pltpu.CompilerParams(vmem_limit_bytes=56 * 1024 * 1024),
    )(skel_upper, cross, pair.reshape(2 * rank, columns))


def solution(mesh):
    in_specs = (
        P(("group", "row"), None),
        P(("group", "row"), None),
        P(("group", "row")),
        P(("group", "row")),
        P("group", None),
    )
    out_specs = (P(("group", "row"), None), P(("group", "row"), None), P(("group", "row"), None))
    return jax.shard_map(local, mesh=mesh, in_specs=in_specs, out_specs=out_specs, check_vma=False)
```
